32 devices in a mesh: dp: 4 (over y, x), peak: 4 (over z), mod: 2 (over core).
Axes of the slice: x: 2, y: 2, z: 4, core: 2. Of those that a mesh axis runs over, the one named last changes fastest.
Arguments:
- hidden_in: bfloat16 [2, 3072, 1024], P('mod', ('dp', 'peak')), parts along dimension 1, may hold values from -31 to 31
- value_bins: int32 [2, 3072], P('mod', ('dp', 'peak')), parts along dimension 1, may hold values from 0 to 50
- mask_flags: int32 [2, 3072], P('mod', ('dp', 'peak')), parts along dimension 1, may hold values 0 or 1
- segment_ids: int32 [2, 16, 192], P('mod', ('dp', 'peak')), parts along dimension 1, may hold values from 0 to 3, never falling along the last dimension, each value on 1 to 96 neighbouring positions
- bin_table: bfloat16 [2, 51, 1024], P('mod'), may hold values from -3 to 3
- mask_vector: bfloat16 [2, 1024], P('mod'), may hold values from -4 to 4
- qkv_weight: bfloat16 [1024, 3072], P('mod'), may hold values from -1 to 1
- out_weight: bfloat16 [1024, 1024], P('mod'), may hold values from -1.5 to 1.5
Outputs:
- update: bfloat16 [2, 3072, 1024], P('mod', ('dp', 'peak')), parts along dimension 1
The draws below stay inside these ranges and needn't reach their ends.
There are 4 independent parts, one for each index of `dp`. The reference program is written for one: setup_inputs(seed, part) draws one part's arguments, and reference() takes and returns one part's arrays. A program takes and returns all parts, laid end to end along the dimension named above; an argument that names none is the same for every part. Nothing has to cross between parts.
Inputs may be any that keep to these rules, and one draw needn't show every extreme that they name: `segment_ids`: in each block of 192 tokens the segments 0 to 3 follow in order, each of 1 to 96 tokens, one of exactly 96.
All inputs are finite; a program needn't handle non-finite values. No bound on the sum of `mask_flags` on one device may be relied on, other than what follows from the above.
Results may differ from the reference program's by a relative error of at most 0.01205.
The reference program's roundings to bfloat16 on the way count: a program that leaves them out, or rounds other values in their place, can miss the bound.
Values may be sent and summed in bfloat16 or wider, within the bound.
No kernel may reach another device: no remote copies, remote signals or barrier semaphores. Data moves between devices by JAX's collectives and lax.ppermute only.
A program may use at most 128 MiB of HBM per device.

```python
import math
import jax
import jax.numpy as jnp
import numpy as np
from jax import lax

D = 1024
H = 16
HD = 64
NBINS = 51
TOK_DEV = 192
SEG_DEV = 4
SEG_MOST = 96
LENGTH = 768
MEMORY = 16
N_PEAK = 4


def draw_hidden_in(key, part):
    shape = (2, LENGTH, D)
    base = jax.random.truncated_normal(jax.random.fold_in(key, 11), -5.0, 5.0, shape, jnp.float32)
    result = base
    return result.astype(jnp.bfloat16)


def draw_qkv_weight(key, part):
    normals = jax.random.truncated_normal(jax.random.fold_in(key, 21), -5.0, 5.0, (D, H, 3, HD), jnp.float32)
    factors = jnp.array([math.sqrt(1.5), math.sqrt(1.5), 1.0], jnp.float32) / math.sqrt(D)
    weights = normals * factors[None, None, :, None]
    return weights.reshape(D, 3 * D).astype(jnp.bfloat16)


def plant(drawn, rng, least, largest):
    dims = drawn.shape
    place = [jax.random.randint(jax.random.fold_in(rng, axis), (), 0, dims[axis]) for axis in range(len(dims))]
    drawn = drawn.at[tuple(place)].set(least)
    longest = dims.index(max(dims))
    place[longest] = (place[longest] + 1) % dims[longest]
    return drawn.at[tuple(place)].set(largest)


def level_of(own_key, shape, shards, least, high):
    loudness, own = 1.0, jax.random.fold_in(own_key, 6)
    for axis_at, shards_of in shards:
        heights = jnp.exp(jax.random.uniform(jax.random.fold_in(own, axis_at), (shards_of,), jnp.float32, least / len(shards), high / len(shards)))
        loudness = loudness * jnp.repeat(heights, shape[axis_at] // shards_of).reshape([-1 if axis == axis_at else 1 for axis in range(len(shape))])
    return loudness


def split_up(number_of, total, reach, slope):
    weights = [(1 << 20) // math.isqrt(grade ** slope) + 1 for grade in range(2, number_of + 1)]
    rest, given = total - reach - (number_of - 1), [1] * (number_of - 1)
    while rest > 0:
        free = [i for i in range(number_of - 1) if given[i] < reach]
        pool, left = sum([weights[i] for i in free]), rest
        for i in free:
            addition = min(reach - given[i], max(1, left * weights[i] // pool), rest)
            given[i] = given[i] + addition
            rest = rest - addition
    return np.array([reach] + given)


def ragged(key, amount, total, reach, slope):
    if amount == 2:
        one = jax.random.randint(key, (), max(1, total - reach), min(reach, total - 1) + 1)
        return jnp.stack([one, total - one])
    tallies = jnp.asarray(split_up(amount, total, reach, slope), jnp.int32)
    couples = (amount - 1) // 2
    giver, sink = tallies[1:1 + 2 * couples:2], tallies[2:2 + 2 * couples:2]
    room = jnp.minimum(giver - 1, reach - sink)
    passed = jax.random.randint(jax.random.fold_in(key, 1), (couples,), 0, 1 << 20) % (room + 1)
    tallies = tallies.at[1:1 + 2 * couples:2].set(giver - passed).at[2:2 + 2 * couples:2].set(sink + passed)
    return tallies[jax.random.permutation(jax.random.fold_in(key, 2), amount)]


def bell_draw(own_key, extent, spread, reach, shards=(), held_as=jnp.bfloat16):
    values = spread * jax.random.normal(own_key, extent, jnp.float32)
    if shards:
        values = values * level_of(own_key, extent, shards, -0.22, 0.18)
    return jnp.clip(values, -reach, reach).astype(held_as)


def setup_inputs(seed: int = 0, part: int = 0) -> dict:
    key_of = jax.random.split(jax.random.key(seed), 9)
    own_keys = jax.random.split(jax.random.fold_in(key_of[8], part), 9)
    return {
        "hidden_in": draw_hidden_in(jax.random.fold_in(jax.random.fold_in(key_of[8], part), 71), part),
        "value_bins": plant(jax.random.randint(own_keys[1], (2, LENGTH), 0, NBINS), jax.random.fold_in(own_keys[1], 1), 0, NBINS - 1).astype(jnp.int32),
        "mask_flags": plant((jax.random.randint(own_keys[2], (2, LENGTH), 0, 100) < 15).astype(jnp.int32), jax.random.fold_in(own_keys[2], 1), 0, 1),
        "segment_ids": jax.vmap(lambda own: jnp.searchsorted(jnp.cumsum(ragged(own, SEG_DEV, TOK_DEV, SEG_MOST, 1)), jnp.arange(TOK_DEV), side="right"))(jax.random.split(own_keys[3], 2 * N_PEAK)).reshape((2, N_PEAK, TOK_DEV)).astype(jnp.int32),
        "bin_table": bell_draw(key_of[4], (2, NBINS, D), 0.5, 3.0, ((0, 2),)),
        "mask_vector": bell_draw(key_of[5], (2, D), 1.0, 4.0, ((0, 2),)),
        "qkv_weight": draw_qkv_weight(jax.random.fold_in(key_of[8], 71), part),
        "out_weight": bell_draw(key_of[7], (D, D), (D // 64) ** -0.5, 1.5, ((0, 2),)),
    }


def embed_tokens(hidden_rows, bin_ids, flag_rows, table, masked_row):
    selector = (bin_ids[:, None] == jnp.arange(NBINS, dtype=jnp.int32)[None, :]).astype(jnp.bfloat16)
    bin_rows = jnp.dot(selector, table, preferred_element_type=jnp.float32)
    chosen = jnp.where(flag_rows[:, None] == 1, masked_row[None, :].astype(jnp.float32), hidden_rows.astype(jnp.float32))
    return (chosen + bin_rows).astype(jnp.bfloat16)


def pool_blocks(key_values, segments):
    blocks = key_values.reshape(N_PEAK, TOK_DEV, 2 * D).astype(jnp.float32)
    selector = (segments[:, None, :] == jnp.arange(SEG_DEV, dtype=jnp.int32)[None, :, None]).astype(jnp.float32)
    sums = jnp.einsum("nst,ntc->nsc", selector, blocks)
    counts = jnp.sum(selector, axis=2)
    pooled = lax.optimization_barrier((sums / counts[:, :, None]).astype(jnp.bfloat16))
    bias = lax.optimization_barrier(jnp.log(counts).astype(jnp.bfloat16))
    return pooled.reshape(MEMORY, H, 2, HD), bias.reshape(MEMORY)


def attend(queries, key_values, pooled, bias):
    score_scale = float(HD) ** -0.5
    key_all = jnp.concatenate([key_values[:, :, 0], pooled[:, :, 0]], axis=0).astype(jnp.float32)
    value_all = jnp.concatenate([key_values[:, :, 1], pooled[:, :, 1]], axis=0).astype(jnp.float32)
    score_bias = jnp.concatenate([jnp.zeros((LENGTH,), jnp.float32), bias.astype(jnp.float32)], axis=0)
    block_size = math.gcd(LENGTH, 256)

    def one_block(query_block):
        scores = jnp.einsum("qhd,khd->qhk", query_block.astype(jnp.float32), key_all) * score_scale
        scores = scores + score_bias[None, None, :]
        row_max = jnp.max(scores, axis=2, keepdims=True)
        weights = jnp.exp(scores - row_max)
        denominator = jnp.sum(weights, axis=2)
        rounded = lax.optimization_barrier(weights.astype(jnp.bfloat16)).astype(jnp.float32)
        numerator = jnp.einsum("qhk,khd->qhd", rounded, value_all)
        return (numerator / denominator[:, :, None]).astype(jnp.bfloat16)

    attended = lax.map(one_block, queries.reshape(LENGTH // block_size, block_size, H, HD))
    return attended.reshape(LENGTH, D)


def reference(hidden_in, value_bins, mask_flags, segment_ids, bin_table, mask_vector, qkv_weight, out_weight):
    query_list = []
    kv_list = []
    pooled_list = []
    bias_list = []
    for modality in range(2):
        embedded = embed_tokens(hidden_in[modality], value_bins[modality], mask_flags[modality], bin_table[modality], mask_vector[modality])
        projected = jnp.dot(embedded, qkv_weight, preferred_element_type=jnp.float32)
        projected = lax.optimization_barrier(projected.astype(jnp.bfloat16)).reshape(LENGTH, H, 3, HD)
        query_list.append(projected[:, :, 0])
        key_values = projected[:, :, 1:3]
        kv_list.append(key_values)
        pooled, bias = pool_blocks(key_values.reshape(LENGTH, 2 * D), segment_ids[modality])
        pooled_list.append(pooled)
        bias_list.append(bias)
    updates = []
    for modality in range(2):
        attended = attend(query_list[modality], kv_list[modality], pooled_list[1 - modality], bias_list[1 - modality])
        updates.append(jnp.dot(attended, out_weight, preferred_element_type=jnp.float32).astype(jnp.bfloat16))
    return jnp.stack(updates, axis=0)
```

```python
import jax
import jax.numpy as jnp
from jax import lax
from jax.experimental import pallas as pl
from jax.experimental.pallas import tpu as pltpu
from jax.sharding import PartitionSpec as P

H = 16
HD = 64
SEG_DEV = 4
PAIRS = H // 2
LANES = 128
BF16 = jnp.bfloat16
F32 = jnp.float32
VMEM_BYTES = 24 * 2**20
NEVER = -1e30


def call(kernel, outs, flops, *operands):
    spec = pl.BlockSpec(memory_space=pltpu.VMEM)
    shapes = [jax.ShapeDtypeStruct(shape, dtype) for shape, dtype in outs]
    return pl.pallas_call(
        kernel,
        out_shape=shapes,
        in_specs=[spec] * len(operands),
        out_specs=[spec] * len(shapes),
        compiler_params=pltpu.CompilerParams(vmem_limit_bytes=VMEM_BYTES),
        cost_estimate=pl.CostEstimate(flops=flops, bytes_accessed=2**20, transcendentals=0),
    )(*operands)


def contract(left, right, left_dim, right_dim):
    return lax.dot_general(
        left, right, (((left_dim,), (right_dim,)), ((), ())), preferred_element_type=F32
    )


def embed_kernel(hidden, bins, flags, segs, table, mask_row, first, second, summary):
    tokens, width = hidden.shape
    half = width // 2
    cut = tokens // 2
    mod = lax.axis_index("mod")
    one_hot = (
        lax.broadcasted_iota(jnp.int32, (table.shape[0], tokens), 0) == bins[...]
    ).astype(BF16)
    flag_rows = jnp.broadcast_to((flags[...] == 1).astype(F32), (LANES, tokens))
    flag_cols = jnp.concatenate([jnp.transpose(flag_rows)] * (half // LANES), axis=1) > 0.5
    seg_rows = lax.broadcasted_iota(jnp.int32, (2 * SEG_DEV, tokens), 0)
    picks = (lax.rem(seg_rows, SEG_DEV) == segs[...]).astype(F32)
    counts = jnp.sum(picks, axis=1, keepdims=True)
    picks = picks.astype(BF16)
    is_mean = lax.broadcasted_iota(jnp.int32, (2 * SEG_DEV, half), 0) < SEG_DEV
    for part in range(2):
        start = pl.multiple_of(lax.rem(mod + part, 2) * half, half)
        bin_rows = contract(one_hot, table[:, pl.ds(start, half)], 0, 0)
        chosen = jnp.where(
            flag_cols,
            mask_row[:, pl.ds(start, half)].astype(F32),
            hidden[:, pl.ds(start, half)].astype(F32),
        )
        embedded = (chosen + bin_rows).astype(BF16)
        columns = pl.ds(part * half, half)
        first[:, columns] = embedded[:cut]
        second[:cut, columns] = embedded[cut:]
        second[cut:, columns] = jnp.zeros((2 * SEG_DEV, half), BF16)
        sums = contract(picks, embedded, 1, 0)
        summary[:, pl.ds((1 - part) * half, half)] = jnp.where(
            is_mean, sums / counts, jnp.log(counts)
        ).astype(BF16)


def arrange_kernel(weight, arranged):
    rows = weight.shape[0]
    width = H * HD
    low = lax.broadcasted_iota(jnp.int32, (rows, LANES), 1) < HD
    for pair in range(PAIRS):
        at = pair * 3 * LANES
        query_key, value_query, key_value = [
            weight[:, at + i * LANES : at + (i + 1) * LANES] for i in range(3)
        ]
        to = pair * LANES
        arranged[:, to : to + LANES] = jnp.where(low, query_key, value_query)
        arranged[:, width + to : width + to + LANES] = jnp.where(low, key_value, query_key)
        arranged[:, 2 * width + to : 2 * width + to + LANES] = jnp.where(
            low, value_query, key_value
        )


def project(rows, weight_here, weight_there, start, stop):
    half = rows.shape[1] // 2
    return contract(rows[:, :half], weight_here[:, start:stop], 1, 0) + contract(
        rows[:, half:], weight_there[:, start:stop], 1, 0
    )


def fold(rows, summary_bias, weight_here, weight_there, turned, old, new):
    width = H * HD
    count = rows.shape[0]
    key = project(rows, weight_here, weight_there, width, 2 * width).astype(BF16)
    value = project(rows, weight_here, weight_there, 2 * width, 3 * width)
    value = jnp.transpose(value).astype(BF16)
    for pair in range(PAIRS):
        columns = slice(pair * LANES, (pair + 1) * LANES)
        scores = contract(key[:, columns], turned[pair], 1, 0)
        if summary_bias is not None:
            edge = count - summary_bias.shape[0]
            scores = jnp.concatenate([scores[:edge], scores[edge:] + summary_bias], axis=0)
        top = jnp.max(scores, axis=0, keepdims=True)
        if old is not None:
            top = jnp.maximum(top, old[0][pair : pair + 1, :])
        weights = jnp.exp(scores - top)
        total = jnp.sum(weights, axis=0, keepdims=True)
        summed = contract(value[columns, :], weights.astype(BF16), 1, 0)
        if old is not None:
            shrink = jnp.exp(old[0][pair : pair + 1, :] - top)
            total = total + shrink * old[1][pair : pair + 1, :]
            summed = summed + shrink * old[2][pair]
        new(pair, top, total, summed)


def bias_of(second):
    edge = second.shape[0] - 2 * SEG_DEV
    tail = second[edge:, :].astype(F32)
    wide = 3 * LANES
    return jnp.concatenate(
        [tail[SEG_DEV:, :wide], jnp.full((SEG_DEV, wide), NEVER, F32)], axis=0
    )


def store_state(top_ref, total_ref, summed_ref):
    def store(pair, top, total, summed):
        top_ref[pair : pair + 1, :] = top
        total_ref[pair : pair + 1, :] = total
        summed_ref[pair] = summed

    return store


def own_kernel(first, second, weight_here, weight_there, turned, top_ref, total_ref, summed_ref):
    cut = first.shape[0]
    width = H * HD
    rows = jnp.concatenate([first[...], second[...]], axis=0)
    query = project(rows[: 2 * cut], weight_here, weight_there, 0, width).astype(BF16)
    query = query.astype(F32) * (float(HD) ** -0.5)
    zeros = jnp.zeros((HD, LANES), F32)
    for pair in range(PAIRS):
        flipped = jnp.transpose(query[:, pair * LANES : (pair + 1) * LANES])
        even, odd = flipped[:HD], flipped[HD:]
        gap = jnp.zeros((HD, HD), F32)
        turned[pair] = jnp.concatenate(
            [
                jnp.concatenate([zeros, odd[:, :LANES], gap, odd[:, LANES:]], axis=1),
                jnp.concatenate([even[:, :LANES], zeros, even[:, LANES:], gap], axis=1),
            ],
            axis=0,
        ).astype(BF16)
    fold(
        rows, bias_of(second), weight_here, weight_there, turned, None,
        store_state(top_ref, total_ref, summed_ref),
    )


def both_kernel(
    first, second, weight_here, weight_there, turned, top_in, total_in, summed_in,
    top_ref, total_ref, summed_ref,
):
    rows = jnp.concatenate([first[...], second[...]], axis=0)
    fold(
        rows, bias_of(second), weight_here, weight_there, turned, (top_in, total_in, summed_in),
        store_state(top_ref, total_ref, summed_ref),
    )


def first_kernel(
    first, weight_here, weight_there, turned, top_in, total_in, summed_in,
    top_ref, total_ref, summed_ref,
):
    fold(
        first[...], None, weight_here, weight_there, turned, (top_in, total_in, summed_in),
        store_state(top_ref, total_ref, summed_ref),
    )


def last_kernel(
    second, weight_here, weight_there, turned, top_in, total_in, summed_in,
    out_here, out_there, update, attended,
):
    def finish(pair, top, total, summed):
        done = summed * (1.0 / total)
        left = jnp.concatenate([done[:HD, :LANES], done[HD:, LANES : 2 * LANES]], axis=0)
        right = jnp.concatenate(
            [done[:HD, 2 * LANES : 2 * LANES + HD], done[HD:, 2 * LANES + HD :]], axis=0
        )
        attended[pair * LANES : (pair + 1) * LANES, :] = jnp.concatenate(
            [left, right], axis=1
        ).astype(BF16)

    fold(
        second[...], bias_of(second), weight_here, weight_there, turned,
        (top_in, total_in, summed_in), finish,
    )
    half = out_here.shape[0]
    mod = lax.axis_index("mod")
    here = attended[pl.ds(pl.multiple_of(mod * half, half), half), :]
    there = attended[pl.ds(pl.multiple_of((1 - mod) * half, half), half), :]
    update[...] = (
        contract(here, out_here[...], 0, 0) + contract(there, out_there[...], 0, 0)
    ).astype(BF16)


def ring_pairs(size):
    order = [0] + list(range(1, size, 2)) + list(reversed(range(2, size, 2)))
    return [(order[i], order[(i + 1) % size]) for i in range(size)]


def swapped(value):
    return lax.ppermute(value, "mod", [(0, 1), (1, 0)])


def shards(
    hidden_in, value_bins, mask_flags, segment_ids, bin_table, mask_vector, qkv_weight, out_weight
):
    tokens, width = hidden_in.shape[1:]
    cut = tokens // 2
    size = lax.axis_size("peak")
    pairs = ring_pairs(size)
    state_shapes = [((PAIRS, 2 * tokens), F32)] * 2 + [((PAIRS, LANES, 2 * tokens), F32)]
    turned_shape = ((PAIRS, LANES, 2 * tokens), BF16)
    first, second, summary = call(
        embed_kernel,
        [((cut, width), BF16), ((cut + 2 * SEG_DEV, width), BF16), ((2 * SEG_DEV, width), BF16)],
        2**28,
        hidden_in[0], value_bins, mask_flags, segment_ids[0], bin_table[0], mask_vector,
    )
    summary = swapped(summary)
    second = lax.dynamic_update_slice(second, summary, (cut, 0))
    (arranged,) = call(arrange_kernel, [(qkv_weight.shape, BF16)], 2**28, qkv_weight)
    weights = (arranged, swapped(arranged))
    out_there = swapped(out_weight)

    turned, *state = call(
        own_kernel, [turned_shape] + state_shapes, 2**31, first, second, *weights
    )
    for step in range(1, size):
        first = lax.ppermute(first, "peak", pairs)
        second = lax.ppermute(second, "peak", pairs)
        if step < size - 1:
            state = call(
                both_kernel, state_shapes, 2**31, first, second, *weights, turned, *state
            )
    state = call(first_kernel, state_shapes, 2**30, first, *weights, turned, *state)
    (update,) = pl.pallas_call(
        last_kernel,
        out_shape=[jax.ShapeDtypeStruct((tokens, width), BF16)],
        in_specs=[pl.BlockSpec(memory_space=pltpu.VMEM)] * 9,
        out_specs=[pl.BlockSpec(memory_space=pltpu.VMEM)],
        scratch_shapes=[pltpu.VMEM((width, tokens), BF16)],
        compiler_params=pltpu.CompilerParams(vmem_limit_bytes=VMEM_BYTES),
        cost_estimate=pl.CostEstimate(flops=2**30, bytes_accessed=2**20, transcendentals=0),
    )(second, *weights, turned, *state, out_weight, out_there)
    return update[None]


def solution(mesh):
    placed = (
        P("mod", ("dp", "peak"), None),
        P("mod", ("dp", "peak")),
        P("mod", ("dp", "peak")),
        P("mod", ("dp", "peak"), None),
        P("mod", None, None),
        P("mod", None),
        P("mod", None),
        P("mod", None),
    )
    return jax.shard_map(
        shards,
        mesh=mesh,
        in_specs=placed,
        out_specs=P("mod", ("dp", "peak"), None),
        check_vma=False,
    )
```

```python
import jax
import jax.numpy as jnp
from jax import lax
from jax.experimental import pallas as pl
from jax.experimental.pallas import tpu as pltpu
from jax.sharding import PartitionSpec as P

H = 16
HD = 64
SEG_DEV = 4
PAIRS = H // 2
LANES = 128
BF16 = jnp.bfloat16
F32 = jnp.float32
VMEM_BYTES = 24 * 2**20
NEVER = -1e30


def call(kernel, outs, flops, *operands):
    spec = pl.BlockSpec(memory_space=pltpu.VMEM)
    shapes = [jax.ShapeDtypeStruct(shape, dtype) for shape, dtype in outs]
    return pl.pallas_call(
        kernel,
        out_shape=shapes,
        in_specs=[spec] * len(operands),
        out_specs=[spec] * len(shapes),
        compiler_params=pltpu.CompilerParams(vmem_limit_bytes=VMEM_BYTES),
        cost_estimate=pl.CostEstimate(flops=flops, bytes_accessed=2**20, transcendentals=0),
    )(*operands)


def contract(left, right, left_dim, right_dim):
    return lax.dot_general(
        left, right, (((left_dim,), (right_dim,)), ((), ())), preferred_element_type=F32
    )


def embed_kernel(*refs):
    sources, (first, second), copies, done = refs[:6], refs[6:8], refs[8:14], refs[14]
    moves = [
        pltpu.make_async_copy(source, copy, done.at[i])
        for i, (source, copy) in enumerate(zip(sources, copies))
    ]
    for move in moves:
        move.start()
    for move in moves:
        move.wait()
    hidden, bins, flags, segs, table, mask_row = copies
    tokens, width = hidden.shape
    half = width // 2
    cut = tokens // 2
    mod = lax.axis_index("mod")
    one_hot = (
        lax.broadcasted_iota(jnp.int32, (table.shape[0], tokens), 0) == bins[...]
    ).astype(BF16)
    flag_rows = jnp.broadcast_to((flags[...] == 1).astype(F32), (LANES, tokens))
    flag_cols = jnp.concatenate([jnp.transpose(flag_rows)] * (half // LANES), axis=1) > 0.5
    seg_rows = lax.broadcasted_iota(jnp.int32, (2 * SEG_DEV, tokens), 0)
    picks = (lax.rem(seg_rows, SEG_DEV) == segs[...]).astype(F32)
    counts = jnp.sum(picks, axis=1, keepdims=True)
    picks = picks.astype(BF16)
    is_mean = lax.broadcasted_iota(jnp.int32, (2 * SEG_DEV, half), 0) < SEG_DEV
    for part in range(2):
        start = pl.multiple_of(lax.rem(mod + part, 2) * half, half)
        bin_rows = contract(one_hot, table[:, pl.ds(start, half)], 0, 0)
        chosen = jnp.where(
            flag_cols,
            mask_row[:, pl.ds(start, half)].astype(F32),
            hidden[:, pl.ds(start, half)].astype(F32),
        )
        embedded = (chosen + bin_rows).astype(BF16)
        columns = pl.ds(part * half, half)
        first[:cut, columns] = embedded[:cut]
        second[:, columns] = embedded[cut:]
        sums = contract(picks, embedded, 1, 0)
        first[cut:, pl.ds((1 - part) * half, half)] = jnp.where(
            is_mean, sums / counts, jnp.log(counts)
        ).astype(BF16)


def arrange_kernel(weight, arranged):
    rows = weight.shape[0]
    width = H * HD
    low = lax.broadcasted_iota(jnp.int32, (rows, LANES), 1) < HD
    for pair in range(PAIRS):
        at = pair * 3 * LANES
        query_key, value_query, key_value = [
            weight[:, at + i * LANES : at + (i + 1) * LANES] for i in range(3)
        ]
        to = pair * LANES
        arranged[:, to : to + LANES] = jnp.where(low, query_key, value_query)
        arranged[:, width + to : width + to + LANES] = jnp.where(low, key_value, query_key)
        arranged[:, 2 * width + to : 2 * width + to + LANES] = jnp.where(
            low, value_query, key_value
        )


def project(rows, weight_here, weight_there, start, stop):
    half = rows.shape[1] // 2
    return contract(rows[:, :half], weight_here[:, start:stop], 1, 0) + contract(
        rows[:, half:], weight_there[:, start:stop], 1, 0
    )


def fold(rows, summary_bias, weight_here, weight_there, turned, old, new):
    width = H * HD
    count = rows.shape[0]
    key = project(rows, weight_here, weight_there, width, 2 * width).astype(BF16)
    low = lax.broadcasted_iota(jnp.int32, (HD, LANES), 1) < HD
    scores, values, folded = {}, {}, {}

    def score(pair):
        found = contract(key[:, pair * LANES : (pair + 1) * LANES], turned[pair], 1, 0)
        if summary_bias is not None:
            edge = count - summary_bias.shape[0]
            found = jnp.concatenate([found[:edge], found[edge:] + summary_bias], axis=0)
        scores[pair] = found

    def value(pair):
        start = 2 * width + pair * LANES
        found = project(rows, weight_here, weight_there, start, start + 2 * LANES)
        found = jnp.transpose(found).astype(BF16)
        values[pair], values[pair + 1] = found[:LANES], found[LANES:]

    def weigh(pair):
        found = scores.pop(pair)
        top = jnp.max(found, axis=0, keepdims=True)
        if old is not None:
            top = jnp.maximum(top, old[0][pair : pair + 1, :])
        weights = jnp.exp(found - top)
        total = jnp.sum(weights, axis=0, keepdims=True)
        shrink = None
        if old is not None:
            shrink = jnp.exp(old[0][pair : pair + 1, :] - top)
            total = total + shrink * old[1][pair : pair + 1, :]
        folded[pair] = (weights.astype(BF16), top, total, shrink)

    def attend(pair):
        weights, top, total, shrink = folded.pop(pair)
        product = contract(values.pop(pair), weights, 1, 0)
        summed = jnp.concatenate(
            [
                product[:HD, :LANES],
                product[HD:, LANES : 2 * LANES],
                jnp.where(low, product[:HD, 2 * LANES :], product[HD:, 2 * LANES :]),
            ],
            axis=1,
        )
        if old is not None:
            summed = summed + shrink * old[2][pair]
        new(pair, top, total, summed)

    score(0)
    score(1)
    for pair in range(PAIRS):
        if pair % 2 == 0:
            value(pair)
        if pair + 2 < PAIRS:
            score(pair + 2)
        weigh(pair)
        if pair >= 1:
            attend(pair - 1)
    attend(PAIRS - 1)


def bias_of(rows):
    edge = rows.shape[0] - 2 * SEG_DEV
    wide = 3 * LANES
    return jnp.concatenate(
        [
            rows[edge:, :wide].astype(F32)[SEG_DEV:],
            jnp.full((SEG_DEV, wide), NEVER, F32),
        ],
        axis=0,
    )


def store_state(top_ref, total_ref, summed_ref):
    def store(pair, top, total, summed):
        top_ref[pair : pair + 1, :] = top
        total_ref[pair : pair + 1, :] = total
        summed_ref[pair] = summed

    return store


def own_kernel(
    first, second, summary, weight_here, weight_there, turned, top_ref, total_ref, summed_ref
):
    cut = second.shape[0]
    width = H * HD
    rows = jnp.concatenate([first[:cut, :], second[...], summary[...]], axis=0)
    query = project(rows[: 2 * cut], weight_here, weight_there, 0, width).astype(BF16)
    query = query.astype(F32) * (float(HD) ** -0.5)
    zeros = jnp.zeros((HD, LANES), F32)
    for pair in range(PAIRS):
        flipped = jnp.transpose(query[:, pair * LANES : (pair + 1) * LANES])
        even, odd = flipped[:HD], flipped[HD:]
        gap = jnp.zeros((HD, HD), F32)
        turned[pair] = jnp.concatenate(
            [
                jnp.concatenate([zeros, odd[:, :LANES], gap, odd[:, LANES:]], axis=1),
                jnp.concatenate([even[:, :LANES], zeros, even[:, LANES:], gap], axis=1),
            ],
            axis=0,
        ).astype(BF16)
    fold(
        rows, bias_of(summary), weight_here, weight_there, turned, None,
        store_state(top_ref, total_ref, summed_ref),
    )


def both_kernel(
    first, second, summary, weight_here, weight_there, turned, top_in, total_in, summed_in,
    top_ref, total_ref, summed_ref,
):
    rows = jnp.concatenate([first[: second.shape[0], :], second[...], summary[...]], axis=0)
    fold(
        rows, bias_of(summary), weight_here, weight_there, turned, (top_in, total_in, summed_in),
        store_state(top_ref, total_ref, summed_ref),
    )


def first_kernel(
    first, weight_here, weight_there, turned, top_in, total_in, summed_in,
    top_ref, total_ref, summed_ref,
):
    fold(
        first[: first.shape[0] - 2 * SEG_DEV, :], None, weight_here, weight_there, turned, (top_in, total_in, summed_in),
        store_state(top_ref, total_ref, summed_ref),
    )


def last_kernel(
    second, summary, weight_here, weight_there, turned, top_in, total_in, summed_in,
    out_here, out_there, update, attended,
):
    def finish(pair, top, total, summed):
        done = (summed * (1.0 / total)).astype(BF16)
        for odd in range(2):
            at = pair * LANES + odd * HD
            rest = 2 * LANES + odd * HD
            attended[at : at + HD, :] = jnp.concatenate(
                [done[:, odd * LANES : (odd + 1) * LANES], done[:, rest : rest + HD]], axis=1
            )

    fold(
        jnp.concatenate([second[...], summary[...]], axis=0), bias_of(summary), weight_here, weight_there, turned,
        (top_in, total_in, summed_in), finish,
    )
    half = out_here.shape[0]
    mod = lax.axis_index("mod")
    here = attended[pl.ds(pl.multiple_of(mod * half, half), half), :]
    there = attended[pl.ds(pl.multiple_of((1 - mod) * half, half), half), :]
    update[...] = (
        contract(here, out_here[...], 0, 0) + contract(there, out_there[...], 0, 0)
    ).astype(BF16)


def ring_pairs(size):
    order = [0] + list(range(1, size, 2)) + list(reversed(range(2, size, 2)))
    return [(order[i], order[(i + 1) % size]) for i in range(size)]


def after(*values):
    return lax.optimization_barrier(values)


def swapped(value):
    return lax.ppermute(value, "mod", [(0, 1), (1, 0)])


def shards(
    hidden_in, value_bins, mask_flags, segment_ids, bin_table, mask_vector, qkv_weight, out_weight
):
    tokens, width = hidden_in.shape[1:]
    cut = tokens // 2
    size = lax.axis_size("peak")
    pairs = ring_pairs(size)
    state_shapes = [((PAIRS, 2 * tokens), F32)] * 2 + [((PAIRS, HD, 2 * tokens), F32)]
    turned_shape = ((PAIRS, LANES, 2 * tokens), BF16)
    operands = (
        hidden_in[0], value_bins, mask_flags, segment_ids[0], bin_table[0], mask_vector,
    )
    vmem = pl.BlockSpec(memory_space=pltpu.VMEM)
    first, second = pl.pallas_call(
        embed_kernel,
        out_shape=[
            jax.ShapeDtypeStruct((rows, width), BF16) for rows in (cut + 2 * SEG_DEV, cut)
        ],
        in_specs=[pl.BlockSpec(memory_space=pltpu.HBM)] * len(operands),
        out_specs=[vmem] * 2,
        scratch_shapes=[pltpu.VMEM(operand.shape, operand.dtype) for operand in operands]
        + [pltpu.SemaphoreType.DMA((len(operands),))],
        compiler_params=pltpu.CompilerParams(vmem_limit_bytes=56 * 2**20),
        cost_estimate=pl.CostEstimate(flops=2**28, bytes_accessed=2**20, transcendentals=0),
    )(*operands)
    weights = [
        call(arrange_kernel, [(weight.shape, BF16)], 2**28, weight)[0]
        for weight in (qkv_weight, swapped(qkv_weight))
    ]
    out_there = swapped(out_weight)

    for step in range(size - 1):
        next_first = lax.ppermute(first, "peak", pairs)
        next_second = lax.ppermute(second, "peak", pairs)
        summary = swapped(first[cut:])
        if step == 0:
            summary, _ = after(summary, next_first)
            turned, *state = call(
                own_kernel, [turned_shape] + state_shapes, 2**31,
                first, second, summary, *weights,
            )
        else:
            if step < size - 2:
                next_first, *state = after(next_first, *state)
            state = call(
                both_kernel, state_shapes, 2**31,
                first, second, summary, *weights, turned, *state,
            )
        first, second = next_first, next_second
    summary = swapped(first[cut:])
    state = call(first_kernel, state_shapes, 2**30, first, *weights, turned, *state)
    (update,) = pl.pallas_call(
        last_kernel,
        out_shape=[jax.ShapeDtypeStruct((tokens, width), BF16)],
        in_specs=[pl.BlockSpec(memory_space=pltpu.VMEM)] * 10,
        out_specs=[pl.BlockSpec(memory_space=pltpu.VMEM)],
        scratch_shapes=[pltpu.VMEM((width, tokens), BF16)],
        compiler_params=pltpu.CompilerParams(vmem_limit_bytes=VMEM_BYTES),
        cost_estimate=pl.CostEstimate(flops=2**30, bytes_accessed=2**20, transcendentals=0),
    )(second, summary, *weights, turned, *state, out_weight, out_there)
    return update[None]


def solution(mesh):
    placed = (
        P("mod", ("dp", "peak"), None),
        P("mod", ("dp", "peak")),
        P("mod", ("dp", "peak")),
        P("mod", ("dp", "peak"), None),
        P("mod", None, None),
        P("mod", None),
        P("mod", None),
        P("mod", None),
    )
    return jax.shard_map(
        shards,
        mesh=mesh,
        in_specs=placed,
        out_specs=P("mod", ("dp", "peak"), None),
        check_vma=False,
    )
```

```python
import jax
import jax.numpy as jnp
from jax import lax
from jax.experimental import pallas as pl
from jax.experimental.pallas import tpu as pltpu
from jax.sharding import PartitionSpec as P

H = 16
HD = 64
SEG_DEV = 4
PAIRS = H // 2
LANES = 128
BF16 = jnp.bfloat16
F32 = jnp.float32
VMEM_BYTES = 24 * 2**20
NEVER = -1e30
COST = (2**28, 2**28)


def call(kernel, outs, flops, *operands):
    spec = pl.BlockSpec(memory_space=pltpu.VMEM)
    shapes = [jax.ShapeDtypeStruct(shape, dtype) for shape, dtype in outs]
    return pl.pallas_call(
        kernel,
        out_shape=shapes,
        in_specs=[spec] * len(operands),
        out_specs=[spec] * len(shapes),
        compiler_params=pltpu.CompilerParams(vmem_limit_bytes=VMEM_BYTES),
        cost_estimate=pl.CostEstimate(flops=flops, bytes_accessed=2**10, transcendentals=0),
    )(*operands)


def contract(left, right, left_dim, right_dim):
    return lax.dot_general(
        left, right, (((left_dim,), (right_dim,)), ((), ())), preferred_element_type=F32
    )


def embed_kernel(*refs):
    sources, (first, second, summary), copies, done = refs[:6], refs[6:9], refs[9:15], refs[15]
    moves = [
        pltpu.make_async_copy(source, copy, done.at[i])
        for i, (source, copy) in enumerate(zip(sources, copies))
    ]
    for move in moves:
        move.start()
    for move in moves:
        move.wait()
    hidden, bins, flags, segs, table, mask_row = copies
    tokens, width = hidden.shape
    half = width // 2
    cut = tokens // 2
    mod = lax.axis_index("mod")
    one_hot = (
        lax.broadcasted_iota(jnp.int32, (table.shape[0], tokens), 0) == bins[...]
    ).astype(BF16)
    flag_rows = jnp.broadcast_to((flags[...] == 1).astype(F32), (LANES, tokens))
    flag_cols = jnp.concatenate([jnp.transpose(flag_rows)] * (half // LANES), axis=1) > 0.5
    seg_rows = lax.broadcasted_iota(jnp.int32, (2 * SEG_DEV, tokens), 0)
    picks = (lax.rem(seg_rows, SEG_DEV) == segs[...]).astype(F32)
    counts = jnp.sum(picks, axis=1, keepdims=True)
    picks = picks.astype(BF16)
    is_mean = lax.broadcasted_iota(jnp.int32, (2 * SEG_DEV, half), 0) < SEG_DEV
    for part in range(2):
        start = pl.multiple_of(lax.rem(mod + part, 2) * half, half)
        bin_rows = contract(one_hot, table[:, pl.ds(start, half)], 0, 0)
        chosen = jnp.where(
            flag_cols,
            mask_row[:, pl.ds(start, half)].astype(F32),
            hidden[:, pl.ds(start, half)].astype(F32),
        )
        embedded = (chosen + bin_rows).astype(BF16)
        columns = pl.ds(part * half, half)
        first[:cut, columns] = embedded[:cut]
        second[:, columns] = embedded[cut:]
        sums = contract(picks, embedded, 1, 0)
        crossed = pl.ds((1 - part) * half, half)
        summary[:, crossed] = jnp.where(is_mean, sums / counts, jnp.log(counts)).astype(BF16)
        first[cut:, crossed] = summary[:, crossed]


def arrange_kernel(weight, arranged):
    rows = weight.shape[0]
    width = H * HD
    low = lax.broadcasted_iota(jnp.int32, (rows, LANES), 1) < HD
    for pair in range(PAIRS):
        at = pair * 3 * LANES
        query_key, value_query, key_value = [
            weight[:, at + i * LANES : at + (i + 1) * LANES] for i in range(3)
        ]
        to = pair * LANES
        arranged[:, to : to + LANES] = jnp.where(low, query_key, value_query)
        arranged[:, width + to : width + to + LANES] = jnp.where(low, key_value, query_key)
        arranged[:, 2 * width + to : 2 * width + to + LANES] = jnp.where(
            low, value_query, key_value
        )


def project(rows, weight_here, weight_there, start, stop):
    half = rows.shape[1] // 2
    return contract(rows[:, :half], weight_here[:, start:stop], 1, 0) + contract(
        rows[:, half:], weight_there[:, start:stop], 1, 0
    )


def fold(rows, summary_bias, weight_here, weight_there, turned, old, new):
    width = H * HD
    count = rows.shape[0]
    key = project(rows, weight_here, weight_there, width, 2 * width).astype(BF16)
    low = lax.broadcasted_iota(jnp.int32, (HD, LANES), 1) < HD
    scores, values, folded = {}, {}, {}

    def score(pair):
        found = contract(key[:, pair * LANES : (pair + 1) * LANES], turned[pair], 1, 0)
        if summary_bias is not None:
            edge = count - summary_bias.shape[0]
            found = jnp.concatenate([found[:edge], found[edge:] + summary_bias], axis=0)
        scores[pair] = found

    def value(pair):
        start = 2 * width + pair * LANES
        found = project(rows, weight_here, weight_there, start, start + 2 * LANES)
        found = jnp.transpose(found).astype(BF16)
        values[pair], values[pair + 1] = found[:LANES], found[LANES:]

    def weigh(pair):
        found = scores.pop(pair)
        top = jnp.max(found, axis=0, keepdims=True)
        if old is not None:
            top = jnp.maximum(top, old[0][pair : pair + 1, :])
        weights = jnp.exp(found - top)
        total = jnp.sum(weights, axis=0, keepdims=True)
        shrink = None
        if old is not None:
            shrink = jnp.exp(old[0][pair : pair + 1, :] - top)
            total = total + shrink * old[1][pair : pair + 1, :]
        folded[pair] = (weights.astype(BF16), top, total, shrink)

    def attend(pair):
        weights, top, total, shrink = folded.pop(pair)
        product = contract(values.pop(pair), weights, 1, 0)
        summed = jnp.concatenate(
            [
                product[:HD, :LANES],
                product[HD:, LANES : 2 * LANES],
                jnp.where(low, product[:HD, 2 * LANES :], product[HD:, 2 * LANES :]),
            ],
            axis=1,
        )
        if old is not None:
            summed = summed + shrink * old[2][pair]
        new(pair, top, total, summed)

    score(0)
    score(1)
    for pair in range(PAIRS):
        if pair % 2 == 0:
            value(pair)
        if pair + 2 < PAIRS:
            score(pair + 2)
        weigh(pair)
        if pair >= 1:
            attend(pair - 1)
    attend(PAIRS - 1)


def bias_of(rows):
    edge = rows.shape[0] - 2 * SEG_DEV
    wide = 3 * LANES
    return jnp.concatenate(
        [
            rows[edge:, :wide].astype(F32)[SEG_DEV:],
            jnp.full((SEG_DEV, wide), NEVER, F32),
        ],
        axis=0,
    )


def store_state(top_ref, total_ref, summed_ref):
    def store(pair, top, total, summed):
        top_ref[pair : pair + 1, :] = top
        total_ref[pair : pair + 1, :] = total
        summed_ref[pair] = summed

    return store


def own_kernel(
    first, second, arrived, summary, weight_here, weight_there,
    turned, top_ref, total_ref, summed_ref,
):
    cut = second.shape[0]
    width = H * HD
    rows = jnp.concatenate(
        [first[:cut, :], second[...], arrived[:cut, :], summary[...]], axis=0
    )
    query = project(rows[: 2 * cut], weight_here, weight_there, 0, width).astype(BF16)
    query = query.astype(F32) * (float(HD) ** -0.5)
    zeros = jnp.zeros((HD, LANES), F32)
    for pair in range(PAIRS):
        flipped = jnp.transpose(query[:, pair * LANES : (pair + 1) * LANES])
        even, odd = flipped[:HD], flipped[HD:]
        gap = jnp.zeros((HD, HD), F32)
        turned[pair] = jnp.concatenate(
            [
                jnp.concatenate([zeros, odd[:, :LANES], gap, odd[:, LANES:]], axis=1),
                jnp.concatenate([even[:, :LANES], zeros, even[:, LANES:], gap], axis=1),
            ],
            axis=0,
        ).astype(BF16)
    fold(
        rows, bias_of(summary), weight_here, weight_there, turned, None,
        store_state(top_ref, total_ref, summed_ref),
    )


def middle_kernel(
    second, first, summary, weight_here, weight_there, turned, top_in, total_in, summed_in,
    top_ref, total_ref, summed_ref,
):
    cut = second.shape[0]
    rows = jnp.concatenate([second[...], first[:cut, :], summary[...]], axis=0)
    fold(
        rows, bias_of(summary), weight_here, weight_there, turned, (top_in, total_in, summed_in),
        store_state(top_ref, total_ref, summed_ref),
    )


def last_kernel(
    second, summary, weight_here, weight_there, turned, top_in, total_in, summed_in,
    out_here, out_there, update, attended,
):
    def finish(pair, top, total, summed):
        done = (summed * (1.0 / total)).astype(BF16)
        for odd in range(2):
            at = pair * LANES + odd * HD
            rest = 2 * LANES + odd * HD
            attended[at : at + HD, :] = jnp.concatenate(
                [done[:, odd * LANES : (odd + 1) * LANES], done[:, rest : rest + HD]], axis=1
            )

    fold(
        jnp.concatenate([second[...], summary[...]], axis=0), bias_of(summary), weight_here, weight_there, turned,
        (top_in, total_in, summed_in), finish,
    )
    half = out_here.shape[0]
    mod = lax.axis_index("mod")
    here = attended[pl.ds(pl.multiple_of(mod * half, half), half), :]
    there = attended[pl.ds(pl.multiple_of((1 - mod) * half, half), half), :]
    update[...] = (
        contract(here, out_here[...], 0, 0) + contract(there, out_there[...], 0, 0)
    ).astype(BF16)


def ring_pairs(size):
    order = [0] + list(range(1, size, 2)) + list(reversed(range(2, size, 2)))
    return [(order[i], order[(i + 1) % size]) for i in range(size)]


def after(*values):
    return lax.optimization_barrier(values)


def swapped(value):
    return lax.ppermute(value, "mod", [(0, 1), (1, 0)])


def shards(
    hidden_in, value_bins, mask_flags, segment_ids, bin_table, mask_vector, qkv_weight, out_weight
):
    tokens, width = hidden_in.shape[1:]
    cut = tokens // 2
    size = lax.axis_size("peak")
    pairs = ring_pairs(size)
    state_shapes = [((PAIRS, 2 * tokens), F32)] * 2 + [((PAIRS, HD, 2 * tokens), F32)]
    turned_shape = ((PAIRS, LANES, 2 * tokens), BF16)
    operands = (
        hidden_in[0], value_bins, mask_flags, segment_ids[0], bin_table[0], mask_vector,
    )
    operands = [pltpu.with_memory_space_constraint(operand, pltpu.HBM) for operand in operands]
    vmem = pl.BlockSpec(memory_space=pltpu.VMEM)
    first, second, summary = pl.pallas_call(
        embed_kernel,
        out_shape=[
            jax.ShapeDtypeStruct((rows, width), BF16) for rows in (cut + 2 * SEG_DEV, cut, 2 * SEG_DEV)
        ],
        in_specs=[pl.BlockSpec(memory_space=pltpu.HBM)] * len(operands),
        out_specs=[vmem] * 3,
        scratch_shapes=[pltpu.VMEM(operand.shape, operand.dtype) for operand in operands]
        + [pltpu.SemaphoreType.DMA((len(operands),))],
        compiler_params=pltpu.CompilerParams(vmem_limit_bytes=VMEM_BYTES),
        cost_estimate=pl.CostEstimate(flops=2**20, bytes_accessed=2**10, transcendentals=0),
    )(*operands)
    weights = [
        call(arrange_kernel, [(weight.shape, BF16)], 2**20, weight)[0]
        for weight in (qkv_weight, swapped(qkv_weight))
    ]
    out_there = swapped(out_weight)

    summary = swapped(summary)
    for step in range(size - 1):
        next_first = lax.ppermute(first, "peak", pairs)
        next_second = lax.ppermute(second, "peak", pairs)
        if step == 0:
            next_first, summary, *weights = after(next_first, summary, *weights)
            turned, *state = call(
                own_kernel, [turned_shape] + state_shapes, COST[0],
                first, second, next_first, summary, *weights,
            )
        else:
            state = call(
                middle_kernel, state_shapes, COST[1],
                second, next_first, summary, *weights, turned, *state,
            )
        if step < size - 2:
            next_second, *state = after(next_second, *state)
        first, second = next_first, next_second
        summary = swapped(first[cut:])
    (update,) = pl.pallas_call(
        last_kernel,
        out_shape=[jax.ShapeDtypeStruct((tokens, width), BF16)],
        in_specs=[pl.BlockSpec(memory_space=pltpu.VMEM)] * 10,
        out_specs=[pl.BlockSpec(memory_space=pltpu.VMEM)],
        scratch_shapes=[pltpu.VMEM((width, tokens), BF16)],
        compiler_params=pltpu.CompilerParams(vmem_limit_bytes=VMEM_BYTES),
        cost_estimate=pl.CostEstimate(flops=2**20, bytes_accessed=2**10, transcendentals=0),
    )(second, summary, *weights, turned, *state, out_weight, out_there)
    return update[None]


def solution(mesh):
    placed = (
        P("mod", ("dp", "peak"), None),
        P("mod", ("dp", "peak")),
        P("mod", ("dp", "peak")),
        P("mod", ("dp", "peak"), None),
        P("mod", None, None),
        P("mod", None),
        P("mod", None),
        P("mod", None),
    )
    return jax.shard_map(
        shards,
        mesh=mesh,
        in_specs=placed,
        out_specs=P("mod", ("dp", "peak"), None),
        check_vma=False,
    )
```

```python
import jax
import jax.numpy as jnp
from jax import lax
from jax.experimental import pallas as pl
from jax.experimental.pallas import tpu as pltpu
from jax.sharding import PartitionSpec as P

H = 16
HD = 64
SEG_DEV = 4
PAIRS = H // 2
LANES = 128
BF16 = jnp.bfloat16
F32 = jnp.float32
VMEM_BYTES = 24 * 2**20
NEVER = -1e30
COST = (2**28, 2**28)


def call(kernel, outs, flops, *operands):
    spec = pl.BlockSpec(memory_space=pltpu.VMEM)
    shapes = [jax.ShapeDtypeStruct(shape, dtype) for shape, dtype in outs]
    return pl.pallas_call(
        kernel,
        out_shape=shapes,
        in_specs=[spec] * len(operands),
        out_specs=[spec] * len(shapes),
        compiler_params=pltpu.CompilerParams(vmem_limit_bytes=VMEM_BYTES),
        cost_estimate=pl.CostEstimate(flops=flops, bytes_accessed=2**10, transcendentals=0),
    )(*operands)


def contract(left, right, left_dim, right_dim):
    return lax.dot_general(
        left, right, (((left_dim,), (right_dim,)), ((), ())), preferred_element_type=F32
    )


def embed_kernel(*refs):
    sources, (first, second, summary), copies, done = refs[:6], refs[6:9], refs[9:15], refs[15]
    moves = [
        pltpu.make_async_copy(source, copy, done.at[i])
        for i, (source, copy) in enumerate(zip(sources, copies))
    ]
    for move in moves:
        move.start()
    for move in moves[1:]:
        move.wait()
    hidden, bins, flags, segs, table, mask_row = copies
    tokens, width = hidden.shape
    half = width // 2
    cut = tokens // 2
    mod = lax.axis_index("mod")
    one_hot = (
        lax.broadcasted_iota(jnp.int32, (table.shape[0], tokens), 0) == bins[...]
    ).astype(BF16)
    flag_rows = jnp.broadcast_to((flags[...] == 1).astype(F32), (LANES, tokens))
    flag_cols = jnp.concatenate([jnp.transpose(flag_rows)] * (half // LANES), axis=1) > 0.5
    seg_rows = lax.broadcasted_iota(jnp.int32, (2 * SEG_DEV, tokens), 0)
    picks = (lax.rem(seg_rows, SEG_DEV) == segs[...]).astype(F32)
    counts = jnp.sum(picks, axis=1, keepdims=True)
    picks = picks.astype(BF16)
    is_mean = lax.broadcasted_iota(jnp.int32, (2 * SEG_DEV, half), 0) < SEG_DEV
    starts = [pl.multiple_of(lax.rem(mod + part, 2) * half, half) for part in range(2)]
    bin_parts = [contract(one_hot, table[:, pl.ds(start, half)], 0, 0) for start in starts]
    moves[0].wait()
    for part, (start, bin_rows) in enumerate(zip(starts, bin_parts)):
        chosen = jnp.where(
            flag_cols,
            mask_row[:, pl.ds(start, half)].astype(F32),
            hidden[:, pl.ds(start, half)].astype(F32),
        )
        embedded = (chosen + bin_rows).astype(BF16)
        columns = pl.ds(part * half, half)
        first[:cut, columns] = embedded[:cut]
        second[:, columns] = embedded[cut:]
        sums = contract(picks, embedded, 1, 0)
        crossed = pl.ds((1 - part) * half, half)
        summary[:, crossed] = jnp.where(is_mean, sums / counts, jnp.log(counts)).astype(BF16)
        first[cut:, crossed] = summary[:, crossed]


def arrange_kernel(weight, arranged):
    rows = weight.shape[0]
    width = H * HD
    low = lax.broadcasted_iota(jnp.int32, (rows, LANES), 1) < HD
    for pair in range(PAIRS):
        at = pair * 3 * LANES
        query_key, value_query, key_value = [
            weight[:, at + i * LANES : at + (i + 1) * LANES] for i in range(3)
        ]
        to = pair * LANES
        arranged[:, to : to + LANES] = jnp.where(low, query_key, value_query)
        arranged[:, width + to : width + to + LANES] = jnp.where(low, key_value, query_key)
        arranged[:, 2 * width + to : 2 * width + to + LANES] = jnp.where(
            low, value_query, key_value
        )


def project(rows, weight_here, weight_there, start, stop):
    half = rows.shape[1] // 2
    return contract(rows[:, :half], weight_here[:, start:stop], 1, 0) + contract(
        rows[:, half:], weight_there[:, start:stop], 1, 0
    )


def fold(rows, summary_bias, weight_here, weight_there, turned, old, new):
    width = H * HD
    count = rows.shape[0]
    key_value = project(rows, weight_here, weight_there, width, 3 * width)
    key = key_value[:, :width].astype(BF16)
    value = jnp.transpose(key_value[:, width:]).astype(BF16)
    low = lax.broadcasted_iota(jnp.int32, (HD, LANES), 1) < HD
    scores, folded = {}, {}

    def score(pair):
        found = contract(key[:, pair * LANES : (pair + 1) * LANES], turned[pair], 1, 0)
        if summary_bias is not None:
            edge = count - summary_bias.shape[0]
            found = jnp.concatenate([found[:edge], found[edge:] + summary_bias], axis=0)
        scores[pair] = found

    def weigh(pair):
        found = scores.pop(pair)
        top = jnp.max(found, axis=0, keepdims=True)
        if old is not None:
            top = jnp.maximum(top, old[0][pair : pair + 1, :])
        weights = jnp.exp(found - top)
        total = jnp.sum(weights, axis=0, keepdims=True)
        shrink = None
        if old is not None:
            shrink = jnp.exp(old[0][pair : pair + 1, :] - top)
            total = total + shrink * old[1][pair : pair + 1, :]
        folded[pair] = (weights.astype(BF16), top, total, shrink)

    def attend(pair):
        weights, top, total, shrink = folded.pop(pair)
        product = contract(value[pair * LANES : (pair + 1) * LANES], weights, 1, 0)
        summed = jnp.concatenate(
            [
                product[:HD, :LANES],
                product[HD:, LANES : 2 * LANES],
                jnp.where(low, product[:HD, 2 * LANES :], product[HD:, 2 * LANES :]),
            ],
            axis=1,
        )
        if old is not None:
            summed = summed + shrink * old[2][pair]
        new(pair, top, total, summed)

    score(0)
    score(1)
    for pair in range(PAIRS):
        if pair + 2 < PAIRS:
            score(pair + 2)
        weigh(pair)
        if pair >= 1:
            attend(pair - 1)
    attend(PAIRS - 1)


def bias_of(rows):
    edge = rows.shape[0] - 2 * SEG_DEV
    wide = 3 * LANES
    return jnp.concatenate(
        [
            rows[edge:, :wide].astype(F32)[SEG_DEV:],
            jnp.full((SEG_DEV, wide), NEVER, F32),
        ],
        axis=0,
    )


def store_state(top_ref, total_ref, summed_ref):
    def store(pair, top, total, summed):
        top_ref[pair : pair + 1, :] = top
        total_ref[pair : pair + 1, :] = total
        summed_ref[pair] = summed

    return store


def own_kernel(
    first, second, arrived, summary, weight_here, weight_there,
    turned, top_ref, total_ref, summed_ref,
):
    cut = second.shape[0]
    width = H * HD
    rows = jnp.concatenate(
        [first[:cut, :], second[...], arrived[:cut, :], summary[...]], axis=0
    )
    query = project(rows[: 2 * cut], weight_here, weight_there, 0, width).astype(BF16)
    query = query.astype(F32) * (float(HD) ** -0.5)
    zeros = jnp.zeros((HD, LANES), F32)
    for pair in range(PAIRS):
        flipped = jnp.transpose(query[:, pair * LANES : (pair + 1) * LANES])
        even, odd = flipped[:HD], flipped[HD:]
        gap = jnp.zeros((HD, HD), F32)
        turned[pair] = jnp.concatenate(
            [
                jnp.concatenate([zeros, odd[:, :LANES], gap, odd[:, LANES:]], axis=1),
                jnp.concatenate([even[:, :LANES], zeros, even[:, LANES:], gap], axis=1),
            ],
            axis=0,
        ).astype(BF16)
    fold(
        rows, bias_of(summary), weight_here, weight_there, turned, None,
        store_state(top_ref, total_ref, summed_ref),
    )


def middle_kernel(
    second, first, summary, weight_here, weight_there, turned, top_in, total_in, summed_in,
    top_ref, total_ref, summed_ref,
):
    cut = second.shape[0]
    rows = jnp.concatenate([second[...], first[:cut, :], summary[...]], axis=0)
    fold(
        rows, bias_of(summary), weight_here, weight_there, turned, (top_in, total_in, summed_in),
        store_state(top_ref, total_ref, summed_ref),
    )


def last_kernel(
    second, summary, weight_here, weight_there, turned, top_in, total_in, summed_in,
    out_here, out_there, update, attended,
):
    def finish(pair, top, total, summed):
        done = (summed * (1.0 / total)).astype(BF16)
        for odd in range(2):
            at = pair * LANES + odd * HD
            rest = 2 * LANES + odd * HD
            attended[at : at + HD, :] = jnp.concatenate(
                [done[:, odd * LANES : (odd + 1) * LANES], done[:, rest : rest + HD]], axis=1
            )

    fold(
        jnp.concatenate([second[...], summary[...]], axis=0), bias_of(summary), weight_here, weight_there, turned,
        (top_in, total_in, summed_in), finish,
    )
    half = out_here.shape[0]
    mod = lax.axis_index("mod")
    here = attended[pl.ds(pl.multiple_of(mod * half, half), half), :]
    there = attended[pl.ds(pl.multiple_of((1 - mod) * half, half), half), :]
    update[...] = (
        contract(here, out_here[...], 0, 0) + contract(there, out_there[...], 0, 0)
    ).astype(BF16)


def ring_pairs(size):
    order = [0] + list(range(1, size, 2)) + list(reversed(range(2, size, 2)))
    return [(order[i], order[(i + 1) % size]) for i in range(size)]


def after(*values):
    return lax.optimization_barrier(values)


def swapped(value):
    return lax.ppermute(value, "mod", [(0, 1), (1, 0)])


def shards(
    hidden_in, value_bins, mask_flags, segment_ids, bin_table, mask_vector, qkv_weight, out_weight
):
    tokens, width = hidden_in.shape[1:]
    cut = tokens // 2
    size = lax.axis_size("peak")
    pairs = ring_pairs(size)
    state_shapes = [((PAIRS, 2 * tokens), F32)] * 2 + [((PAIRS, HD, 2 * tokens), F32)]
    turned_shape = ((PAIRS, LANES, 2 * tokens), BF16)
    operands = (
        hidden_in[0], value_bins, mask_flags, segment_ids[0], bin_table[0], mask_vector,
    )
    operands = [pltpu.with_memory_space_constraint(operand, pltpu.HBM) for operand in operands]
    vmem = pl.BlockSpec(memory_space=pltpu.VMEM)
    first, second, summary = pl.pallas_call(
        embed_kernel,
        out_shape=[
            jax.ShapeDtypeStruct((rows, width), BF16) for rows in (cut + 2 * SEG_DEV, cut, 2 * SEG_DEV)
        ],
        in_specs=[pl.BlockSpec(memory_space=pltpu.HBM)] * len(operands),
        out_specs=[vmem] * 3,
        scratch_shapes=[pltpu.VMEM(operand.shape, operand.dtype) for operand in operands]
        + [pltpu.SemaphoreType.DMA((len(operands),))],
        compiler_params=pltpu.CompilerParams(vmem_limit_bytes=VMEM_BYTES),
        cost_estimate=pl.CostEstimate(flops=2**20, bytes_accessed=2**10, transcendentals=0),
    )(*operands)
    weights = [
        call(arrange_kernel, [(weight.shape, BF16)], 2**20, weight)[0]
        for weight in (qkv_weight, swapped(qkv_weight))
    ]
    out_there = swapped(out_weight)

    summary = swapped(summary)
    for step in range(size - 1):
        next_first = lax.ppermute(first, "peak", pairs)
        next_second = lax.ppermute(second, "peak", pairs)
        if step == 0:
            next_first, summary, *weights = after(next_first, summary, *weights)
            turned, *state = call(
                own_kernel, [turned_shape] + state_shapes, COST[0],
                first, second, next_first, summary, *weights,
            )
        else:
            state = call(
                middle_kernel, state_shapes, COST[1],
                second, next_first, summary, *weights, turned, *state,
            )
        if step < size - 2:
            next_second, *state = after(next_second, *state)
        first, second = next_first, next_second
        summary = swapped(first[cut:])
    (update,) = pl.pallas_call(
        last_kernel,
        out_shape=[jax.ShapeDtypeStruct((tokens, width), BF16)],
        in_specs=[pl.BlockSpec(memory_space=pltpu.VMEM)] * 10,
        out_specs=[pl.BlockSpec(memory_space=pltpu.VMEM)],
        scratch_shapes=[pltpu.VMEM((width, tokens), BF16)],
        compiler_params=pltpu.CompilerParams(vmem_limit_bytes=VMEM_BYTES),
        cost_estimate=pl.CostEstimate(flops=2**20, bytes_accessed=2**10, transcendentals=0),
    )(second, summary, *weights, turned, *state, out_weight, out_there)
    return update[None]


def solution(mesh):
    placed = (
        P("mod", ("dp", "peak"), None),
        P("mod", ("dp", "peak")),
        P("mod", ("dp", "peak")),
        P("mod", ("dp", "peak"), None),
        P("mod", None, None),
        P("mod", None),
        P("mod", None),
        P("mod", None),
    )
    return jax.shard_map(
        shards,
        mesh=mesh,
        in_specs=placed,
        out_specs=P("mod", ("dp", "peak"), None),
        check_vma=False,
    )
```

```python
import jax
import jax.numpy as jnp
from jax import lax
from jax.experimental import pallas as pl
from jax.experimental.pallas import tpu as pltpu
from jax.sharding import PartitionSpec as P

H = 16
HD = 64
SEG_DEV = 4
PAIRS = H // 2
LANES = 128
BF16 = jnp.bfloat16
F32 = jnp.float32
VMEM_BYTES = 24 * 2**20
NEVER = -1e30
COST = (2**28, 2**28)


def call(kernel, outs, flops, *operands):
    spec = pl.BlockSpec(memory_space=pltpu.VMEM)
    shapes = [jax.ShapeDtypeStruct(shape, dtype) for shape, dtype in outs]
    return pl.pallas_call(
        kernel,
        out_shape=shapes,
        in_specs=[spec] * len(operands),
        out_specs=[spec] * len(shapes),
        compiler_params=pltpu.CompilerParams(vmem_limit_bytes=VMEM_BYTES),
        cost_estimate=pl.CostEstimate(flops=flops, bytes_accessed=2**10, transcendentals=0),
    )(*operands)


def contract(left, right, left_dim, right_dim):
    return lax.dot_general(
        left, right, (((left_dim,), (right_dim,)), ((), ())), preferred_element_type=F32
    )


def embed_kernel(*refs):
    sources, (first, second, summary), copies, done = refs[:6], refs[6:9], refs[9:15], refs[15]
    moves = [
        pltpu.make_async_copy(source, copy, done.at[i])
        for i, (source, copy) in enumerate(zip(sources, copies))
    ]
    for move in moves:
        move.start()
    for move in moves[1:]:
        move.wait()
    hidden, bins, flags, segs, table, mask_row = copies
    tokens, width = hidden.shape
    half = width // 2
    cut = tokens // 2
    mod = lax.axis_index("mod")
    one_hot = (
        lax.broadcasted_iota(jnp.int32, (table.shape[0], tokens), 0) == bins[...]
    ).astype(BF16)
    flag_rows = jnp.broadcast_to((flags[...] == 1).astype(F32), (LANES, tokens))
    flag_cols = jnp.concatenate([jnp.transpose(flag_rows)] * (half // LANES), axis=1) > 0.5
    seg_rows = lax.broadcasted_iota(jnp.int32, (2 * SEG_DEV, tokens), 0)
    picks = (lax.rem(seg_rows, SEG_DEV) == segs[...]).astype(F32)
    counts = jnp.sum(picks, axis=1, keepdims=True)
    picks = picks.astype(BF16)
    is_mean = lax.broadcasted_iota(jnp.int32, (2 * SEG_DEV, half), 0) < SEG_DEV
    starts = [pl.multiple_of(lax.rem(mod + part, 2) * half, half) for part in range(2)]
    bin_parts = [contract(one_hot, table[:, pl.ds(start, half)], 0, 0) for start in starts]
    means = []
    moves[0].wait()
    for part, (start, bin_rows) in enumerate(zip(starts, bin_parts)):
        chosen = jnp.where(
            flag_cols,
            mask_row[:, pl.ds(start, half)].astype(F32),
            hidden[:, pl.ds(start, half)].astype(F32),
        )
        embedded = (chosen + bin_rows).astype(BF16)
        columns = pl.ds(part * half, half)
        for tile in range(half // LANES):
            at = (part * (half // LANES) + tile) * cut
            first[at : at + cut, :] = embedded[:cut, tile * LANES : (tile + 1) * LANES]
        second[:, columns] = embedded[cut:]
        means.append(contract(picks, embedded, 1, 0) / counts)
    both = jnp.where(is_mean, means[1], means[0])
    bias = jnp.broadcast_to(jnp.log(counts), (2 * SEG_DEV, LANES))
    tiles = [both[:, at : at + LANES] for at in range(0, half, LANES)]
    packed = jnp.concatenate(tiles + [bias], axis=0).astype(BF16)
    summary[...] = packed
    first[first.shape[0] - packed.shape[0] :, :] = packed


def arrange_kernel(weight, arranged):
    rows = weight.shape[0]
    width = H * HD
    low = lax.broadcasted_iota(jnp.int32, (rows, LANES), 1) < HD
    for pair in range(PAIRS):
        at = pair * 3 * LANES
        query_key, value_query, key_value = [
            weight[:, at + i * LANES : at + (i + 1) * LANES] for i in range(3)
        ]
        to = pair * LANES
        arranged[:, to : to + LANES] = jnp.where(low, query_key, value_query)
        arranged[:, width + to : width + to + LANES] = jnp.where(low, key_value, query_key)
        arranged[:, 2 * width + to : 2 * width + to + LANES] = jnp.where(
            low, value_query, key_value
        )


def project(rows, weight_here, weight_there, start, stop):
    half = rows.shape[1] // 2
    return contract(rows[:, :half], weight_here[:, start:stop], 1, 0) + contract(
        rows[:, half:], weight_there[:, start:stop], 1, 0
    )


def fold(rows, summary_bias, weight_here, weight_there, turned, old, new):
    width = H * HD
    count = rows.shape[0]
    key_value = project(rows, weight_here, weight_there, width, 3 * width)
    key = key_value[:, :width].astype(BF16)
    value = jnp.transpose(key_value[:, width:]).astype(BF16)
    low = lax.broadcasted_iota(jnp.int32, (HD, LANES), 1) < HD
    scores, folded = {}, {}

    def score(pair):
        found = contract(key[:, pair * LANES : (pair + 1) * LANES], turned[pair], 1, 0)
        if summary_bias is not None:
            edge = count - summary_bias.shape[0]
            found = jnp.concatenate([found[:edge], found[edge:] + summary_bias], axis=0)
        scores[pair] = found

    def weigh(pair):
        found = scores.pop(pair)
        top = jnp.max(found, axis=0, keepdims=True)
        if old is not None:
            top = jnp.maximum(top, old[0][pair : pair + 1, :])
        weights = jnp.exp(found - top)
        total = jnp.sum(weights, axis=0, keepdims=True)
        shrink = None
        if old is not None:
            shrink = jnp.exp(old[0][pair : pair + 1, :] - top)
            total = total + shrink * old[1][pair : pair + 1, :]
        folded[pair] = (weights.astype(BF16), top, total, shrink)

    def attend(pair):
        weights, top, total, shrink = folded.pop(pair)
        product = contract(value[pair * LANES : (pair + 1) * LANES], weights, 1, 0)
        summed = jnp.concatenate(
            [
                product[:HD, :LANES],
                product[HD:, LANES : 2 * LANES],
                jnp.where(low, product[:HD, 2 * LANES :], product[HD:, 2 * LANES :]),
            ],
            axis=1,
        )
        if old is not None:
            summed = summed + shrink * old[2][pair]
        new(pair, top, total, summed)

    score(0)
    score(1)
    for pair in range(PAIRS):
        if pair + 2 < PAIRS:
            score(pair + 2)
        weigh(pair)
        if pair >= 1:
            attend(pair - 1)
    attend(PAIRS - 1)


def tokens_of(first, width):
    count = width // LANES
    cut = (first.shape[0] - (count // 2 + 1) * 2 * SEG_DEV) // count
    return jnp.concatenate([first[tile * cut : (tile + 1) * cut, :] for tile in range(count)], axis=1)


def summaries_of(packed):
    rows = 2 * SEG_DEV
    tiles = packed[...].astype(F32)
    tiles = [tiles[at : at + rows] for at in range(0, packed.shape[0], rows)]
    turned = [jnp.concatenate([tile[SEG_DEV:], tile[:SEG_DEV]], axis=0) for tile in tiles[:-1]]
    means = jnp.concatenate(tiles[:-1] + turned, axis=1).astype(BF16)
    is_key = lax.broadcasted_iota(jnp.int32, (rows, 3 * LANES), 0) < SEG_DEV
    return means, jnp.where(is_key, jnp.concatenate([tiles[-1]] * 3, axis=1), NEVER)


def store_state(top_ref, total_ref, summed_ref):
    def store(pair, top, total, summed):
        top_ref[pair : pair + 1, :] = top
        total_ref[pair : pair + 1, :] = total
        summed_ref[pair] = summed

    return store


def own_kernel(
    first, second, arrived, summary, weight_here, weight_there,
    turned, top_ref, total_ref, summed_ref,
):
    cut, width = second.shape
    means, bias = summaries_of(summary)
    rows = jnp.concatenate(
        [tokens_of(first, width), second[...], tokens_of(arrived, width), means], axis=0
    )
    query = project(rows[: 2 * cut], weight_here, weight_there, 0, width).astype(BF16)
    query = query.astype(F32) * (float(HD) ** -0.5)
    zeros = jnp.zeros((HD, LANES), F32)
    for pair in range(PAIRS):
        flipped = jnp.transpose(query[:, pair * LANES : (pair + 1) * LANES])
        even, odd = flipped[:HD], flipped[HD:]
        gap = jnp.zeros((HD, HD), F32)
        turned[pair] = jnp.concatenate(
            [
                jnp.concatenate([zeros, odd[:, :LANES], gap, odd[:, LANES:]], axis=1),
                jnp.concatenate([even[:, :LANES], zeros, even[:, LANES:], gap], axis=1),
            ],
            axis=0,
        ).astype(BF16)
    fold(
        rows, bias, weight_here, weight_there, turned, None,
        store_state(top_ref, total_ref, summed_ref),
    )


def middle_kernel(
    second, first, summary, weight_here, weight_there, turned, top_in, total_in, summed_in,
    top_ref, total_ref, summed_ref,
):
    means, bias = summaries_of(summary)
    rows = jnp.concatenate([second[...], tokens_of(first, second.shape[1]), means], axis=0)
    fold(
        rows, bias, weight_here, weight_there, turned, (top_in, total_in, summed_in),
        store_state(top_ref, total_ref, summed_ref),
    )


def last_kernel(
    second, summary, weight_here, weight_there, turned, top_in, total_in, summed_in,
    out_here, out_there, update, attended,
):
    def finish(pair, top, total, summed):
        done = (summed * (1.0 / total)).astype(BF16)
        for odd in range(2):
            at = pair * LANES + odd * HD
            rest = 2 * LANES + odd * HD
            attended[at : at + HD, :] = jnp.concatenate(
                [done[:, odd * LANES : (odd + 1) * LANES], done[:, rest : rest + HD]], axis=1
            )

    means, bias = summaries_of(summary)
    fold(
        jnp.concatenate([second[...], means], axis=0), bias, weight_here, weight_there, turned,
        (top_in, total_in, summed_in), finish,
    )
    half = out_here.shape[0]
    mod = lax.axis_index("mod")
    here = attended[pl.ds(pl.multiple_of(mod * half, half), half), :]
    there = attended[pl.ds(pl.multiple_of((1 - mod) * half, half), half), :]
    update[...] = (
        contract(here, out_here[...], 0, 0) + contract(there, out_there[...], 0, 0)
    ).astype(BF16)


def ring_pairs(size):
    order = [0] + list(range(1, size, 2)) + list(reversed(range(2, size, 2)))
    return [(order[i], order[(i + 1) % size]) for i in range(size)]


def after(*values):
    return lax.optimization_barrier(values)


def swapped(value):
    return lax.ppermute(value, "mod", [(0, 1), (1, 0)])


def shards(
    hidden_in, value_bins, mask_flags, segment_ids, bin_table, mask_vector, qkv_weight, out_weight
):
    tokens, width = hidden_in.shape[1:]
    cut = tokens // 2
    extra = (width // LANES // 2 + 1) * 2 * SEG_DEV
    size = lax.axis_size("peak")
    pairs = ring_pairs(size)
    state_shapes = [((PAIRS, 2 * tokens), F32)] * 2 + [((PAIRS, HD, 2 * tokens), F32)]
    turned_shape = ((PAIRS, LANES, 2 * tokens), BF16)
    operands = (
        hidden_in[0], value_bins, mask_flags, segment_ids[0], bin_table[0], mask_vector,
    )
    operands = [pltpu.with_memory_space_constraint(operand, pltpu.HBM) for operand in operands]
    vmem = pl.BlockSpec(memory_space=pltpu.VMEM)
    first, second, summary = pl.pallas_call(
        embed_kernel,
        out_shape=[
            jax.ShapeDtypeStruct((cut * width // LANES + extra, LANES), BF16),
            jax.ShapeDtypeStruct((tokens - cut, width), BF16),
            jax.ShapeDtypeStruct((extra, LANES), BF16),
        ],
        in_specs=[pl.BlockSpec(memory_space=pltpu.HBM)] * len(operands),
        out_specs=[vmem] * 3,
        scratch_shapes=[pltpu.VMEM(operand.shape, operand.dtype) for operand in operands]
        + [pltpu.SemaphoreType.DMA((len(operands),))],
        compiler_params=pltpu.CompilerParams(vmem_limit_bytes=VMEM_BYTES),
        cost_estimate=pl.CostEstimate(flops=2**20, bytes_accessed=2**10, transcendentals=0),
    )(*operands)
    weights = [
        call(arrange_kernel, [(weight.shape, BF16)], 2**20, weight)[0]
        for weight in (qkv_weight, swapped(qkv_weight))
    ]
    out_there = swapped(out_weight)

    summary = swapped(summary)
    for step in range(size - 1):
        next_first = lax.ppermute(first, "peak", pairs)
        next_second = lax.ppermute(second, "peak", pairs)
        if step == 0:
            next_first, summary, *weights = after(next_first, summary, *weights)
            turned, *state = call(
                own_kernel, [turned_shape] + state_shapes, COST[0],
                first, second, next_first, summary, *weights,
            )
        else:
            state = call(
                middle_kernel, state_shapes, COST[1],
                second, next_first, summary, *weights, turned, *state,
            )
        if step < size - 2:
            next_second, *state = after(next_second, *state)
        first, second = next_first, next_second
        summary = swapped(first[first.shape[0] - extra :])
    (update,) = pl.pallas_call(
        last_kernel,
        out_shape=[jax.ShapeDtypeStruct((tokens, width), BF16)],
        in_specs=[pl.BlockSpec(memory_space=pltpu.VMEM)] * 10,
        out_specs=[pl.BlockSpec(memory_space=pltpu.VMEM)],
        scratch_shapes=[pltpu.VMEM((width, tokens), BF16)],
        compiler_params=pltpu.CompilerParams(vmem_limit_bytes=VMEM_BYTES),
        cost_estimate=pl.CostEstimate(flops=2**20, bytes_accessed=2**10, transcendentals=0),
    )(second, summary, *weights, turned, *state, out_weight, out_there)
    return update[None]


def solution(mesh):
    placed = (
        P("mod", ("dp", "peak"), None),
        P("mod", ("dp", "peak")),
        P("mod", ("dp", "peak")),
        P("mod", ("dp", "peak"), None),
        P("mod", None, None),
        P("mod", None),
        P("mod", None),
        P("mod", None),
    )
    return jax.shard_map(
        shards,
        mesh=mesh,
        in_specs=placed,
        out_specs=P("mod", ("dp", "peak"), None),
        check_vma=False,
    )
```

```python
import jax
import jax.numpy as jnp
from jax import lax
from jax.experimental import pallas as pl
from jax.experimental.pallas import tpu as pltpu
from jax.sharding import PartitionSpec as P

H = 16
HD = 64
SEG_DEV = 4
PAIRS = H // 2
LANES = 128
BF16 = jnp.bfloat16
F32 = jnp.float32
VMEM_BYTES = 24 * 2**20
NEVER = -1e30
COST = (2**28, 2**28)


def call(kernel, outs, flops, *operands):
    spec = pl.BlockSpec(memory_space=pltpu.VMEM)
    shapes = [jax.ShapeDtypeStruct(shape, dtype) for shape, dtype in outs]
    return pl.pallas_call(
        kernel,
        out_shape=shapes,
        in_specs=[spec] * len(operands),
        out_specs=[spec] * len(shapes),
        compiler_params=pltpu.CompilerParams(vmem_limit_bytes=VMEM_BYTES),
        cost_estimate=pl.CostEstimate(flops=flops, bytes_accessed=2**10, transcendentals=0),
    )(*operands)


def contract(left, right, left_dim, right_dim):
    return lax.dot_general(
        left, right, (((left_dim,), (right_dim,)), ((), ())), preferred_element_type=F32
    )


def embed_kernel(*refs):
    sources, (first, second, summary), copies, done = refs[:6], refs[6:9], refs[9:15], refs[15]
    moves = [
        pltpu.make_async_copy(source, copy, done.at[i])
        for i, (source, copy) in enumerate(zip(sources, copies))
    ]
    for move in moves:
        move.start()
    for move in moves[1:]:
        move.wait()
    hidden, bins, flags, segs, table, mask_row = copies
    tokens, width = hidden.shape
    half = width // 2
    cut = tokens // 2
    mod = lax.axis_index("mod")
    one_hot = (
        lax.broadcasted_iota(jnp.int32, (table.shape[0], tokens), 0) == bins[...]
    ).astype(BF16)
    flag_rows = jnp.broadcast_to((flags[...] == 1).astype(F32), (LANES, tokens))
    flag_cols = jnp.concatenate([jnp.transpose(flag_rows)] * (half // LANES), axis=1) > 0.5
    seg_rows = lax.broadcasted_iota(jnp.int32, (2 * SEG_DEV, tokens), 0)
    picks = (lax.rem(seg_rows, SEG_DEV) == segs[...]).astype(F32)
    counts = jnp.sum(picks, axis=1, keepdims=True)
    picks = picks.astype(BF16)
    is_mean = lax.broadcasted_iota(jnp.int32, (2 * SEG_DEV, half), 0) < SEG_DEV
    starts = [pl.multiple_of(lax.rem(mod + part, 2) * half, half) for part in range(2)]
    bin_parts = [contract(one_hot, table[:, pl.ds(start, half)], 0, 0) for start in starts]
    means = []
    moves[0].wait()
    for part, (start, bin_rows) in enumerate(zip(starts, bin_parts)):
        chosen = jnp.where(
            flag_cols,
            mask_row[:, pl.ds(start, half)].astype(F32),
            hidden[:, pl.ds(start, half)].astype(F32),
        )
        embedded = (chosen + bin_rows).astype(BF16)
        columns = pl.ds(part * half, half)
        for tile in range(half // LANES):
            at = (part * (half // LANES) + tile) * cut
            first[at : at + cut, :] = embedded[:cut, tile * LANES : (tile + 1) * LANES]
        second[:, columns] = embedded[cut:]
        means.append(contract(picks, embedded, 1, 0) / counts)
    both = jnp.where(is_mean, means[1], means[0])
    bias = jnp.broadcast_to(jnp.log(counts), (2 * SEG_DEV, LANES))
    tiles = [both[:, at : at + LANES] for at in range(0, half, LANES)]
    packed = jnp.concatenate(tiles + [bias], axis=0).astype(BF16)
    summary[...] = packed
    first[first.shape[0] - packed.shape[0] :, :] = packed


def arrange_kernel(weight, arranged):
    rows = weight.shape[0]
    width = H * HD
    low = lax.broadcasted_iota(jnp.int32, (rows, LANES), 1) < HD
    for pair in range(PAIRS):
        at = pair * 3 * LANES
        query_key, value_query, key_value = [
            weight[:, at + i * LANES : at + (i + 1) * LANES] for i in range(3)
        ]
        to = pair * LANES
        arranged[:, to : to + LANES] = jnp.where(low, query_key, value_query)
        arranged[:, width + to : width + to + LANES] = jnp.where(low, key_value, query_key)
        arranged[:, 2 * width + to : 2 * width + to + LANES] = jnp.where(
            low, value_query, key_value
        )


def project(rows, weight_here, weight_there, start, stop):
    half = rows.shape[1] // 2
    return contract(rows[:, :half], weight_here[:, start:stop], 1, 0) + contract(
        rows[:, half:], weight_there[:, start:stop], 1, 0
    )


def fold(rows, summary_bias, weight_here, weight_there, turned, old, new):
    width = H * HD
    count = rows.shape[0]
    key_value = project(rows, weight_here, weight_there, width, 3 * width)
    key = key_value[:, :width].astype(BF16)
    value = jnp.transpose(key_value[:, width:]).astype(BF16)
    low = lax.broadcasted_iota(jnp.int32, (HD, LANES), 1) < HD
    scores, folded = {}, {}

    def score(pair):
        found = contract(key[:, pair * LANES : (pair + 1) * LANES], turned[pair], 1, 0)
        if summary_bias is not None:
            edge = count - summary_bias.shape[0]
            found = jnp.concatenate([found[:edge], found[edge:] + summary_bias], axis=0)
        scores[pair] = found

    def weigh(pair):
        found = scores.pop(pair)
        top = jnp.max(found, axis=0, keepdims=True)
        if old is not None:
            top = jnp.maximum(top, old[0][pair : pair + 1, :])
        weights = jnp.exp(found - top)
        total = jnp.sum(weights, axis=0, keepdims=True)
        shrink = None
        if old is not None:
            shrink = jnp.exp(old[0][pair : pair + 1, :] - top)
            total = total + shrink * old[1][pair : pair + 1, :]
        folded[pair] = (weights.astype(BF16), top, total, shrink)

    def attend(pair):
        weights, top, total, shrink = folded.pop(pair)
        product = contract(value[pair * LANES : (pair + 1) * LANES], weights, 1, 0)
        summed = jnp.concatenate(
            [
                product[:HD, :LANES],
                product[HD:, LANES : 2 * LANES],
                jnp.where(low, product[:HD, 2 * LANES :], product[HD:, 2 * LANES :]),
            ],
            axis=1,
        )
        if old is not None:
            summed = summed + shrink * old[2][pair]
        new(pair, top, total, summed)

    score(0)
    score(1)
    for pair in range(PAIRS):
        if pair + 2 < PAIRS:
            score(pair + 2)
        weigh(pair)
        if pair >= 1:
            attend(pair - 1)
    attend(PAIRS - 1)


def tokens_of(first, width):
    count = width // LANES
    cut = (first.shape[0] - (count // 2 + 1) * 2 * SEG_DEV) // count
    return jnp.concatenate([first[tile * cut : (tile + 1) * cut, :] for tile in range(count)], axis=1)


def summaries_of(packed):
    rows = 2 * SEG_DEV
    tiles = packed[...].astype(F32)
    tiles = [tiles[at : at + rows] for at in range(0, packed.shape[0], rows)]
    turned = [jnp.concatenate([tile[SEG_DEV:], tile[:SEG_DEV]], axis=0) for tile in tiles[:-1]]
    means = jnp.concatenate(tiles[:-1] + turned, axis=1).astype(BF16)
    is_key = lax.broadcasted_iota(jnp.int32, (rows, 3 * LANES), 0) < SEG_DEV
    return means, jnp.where(is_key, jnp.concatenate([tiles[-1]] * 3, axis=1), NEVER)


def store_state(top_ref, total_ref, summed_ref):
    def store(pair, top, total, summed):
        top_ref[pair : pair + 1, :] = top
        total_ref[pair : pair + 1, :] = total
        summed_ref[pair] = summed

    return store


def own_kernel(
    first, second, arrived, summary, weight_here, weight_there,
    turned, top_ref, total_ref, summed_ref,
):
    cut, width = second.shape
    means, bias = summaries_of(summary)
    rows = jnp.concatenate(
        [tokens_of(first, width), second[...], tokens_of(arrived, width), means], axis=0
    )
    query = project(rows[: 2 * cut], weight_here, weight_there, 0, width).astype(BF16)
    query = query.astype(F32) * (float(HD) ** -0.5)
    zeros = jnp.zeros((HD, LANES), F32)
    for pair in range(PAIRS):
        flipped = jnp.transpose(query[:, pair * LANES : (pair + 1) * LANES])
        even, odd = flipped[:HD], flipped[HD:]
        gap = jnp.zeros((HD, HD), F32)
        turned[pair] = jnp.concatenate(
            [
                jnp.concatenate([zeros, odd[:, :LANES], gap, odd[:, LANES:]], axis=1),
                jnp.concatenate([even[:, :LANES], zeros, even[:, LANES:], gap], axis=1),
            ],
            axis=0,
        ).astype(BF16)
    fold(
        rows, bias, weight_here, weight_there, turned, None,
        store_state(top_ref, total_ref, summed_ref),
    )


def middle_kernel(
    second, first, summary, weight_here, weight_there, turned, top_in, total_in, summed_in,
    top_ref, total_ref, summed_ref,
):
    means, bias = summaries_of(summary)
    rows = jnp.concatenate([second[...], tokens_of(first, second.shape[1]), means], axis=0)
    fold(
        rows, bias, weight_here, weight_there, turned, (top_in, total_in, summed_in),
        store_state(top_ref, total_ref, summed_ref),
    )


def last_kernel(
    second, summary, weight_here, weight_there, turned, top_in, total_in, summed_in,
    out_here, out_there, update, attended,
):
    def finish(pair, top, total, summed):
        done = (summed * (1.0 / total)).astype(BF16)
        for odd in range(2):
            at = pair * LANES + odd * HD
            rest = 2 * LANES + odd * HD
            attended[at : at + HD, :] = jnp.concatenate(
                [done[:, odd * LANES : (odd + 1) * LANES], done[:, rest : rest + HD]], axis=1
            )

    means, bias = summaries_of(summary)
    fold(
        jnp.concatenate([second[...], means], axis=0), bias, weight_here, weight_there, turned,
        (top_in, total_in, summed_in), finish,
    )
    half = out_here.shape[0]
    mod = lax.axis_index("mod")
    here = attended[pl.ds(pl.multiple_of(mod * half, half), half), :]
    there = attended[pl.ds(pl.multiple_of((1 - mod) * half, half), half), :]
    update[...] = (
        contract(here, out_here[...], 0, 0) + contract(there, out_there[...], 0, 0)
    ).astype(BF16)


def ring_pairs(size):
    order = [0] + list(range(1, size, 2)) + list(reversed(range(2, size, 2)))
    return [(order[(i + 1) % size], order[i]) for i in range(size)]


def after(*values):
    return lax.optimization_barrier(values)


def swapped(value):
    return lax.ppermute(value, "mod", [(0, 1), (1, 0)])


def shards(
    hidden_in, value_bins, mask_flags, segment_ids, bin_table, mask_vector, qkv_weight, out_weight
):
    tokens, width = hidden_in.shape[1:]
    cut = tokens // 2
    extra = (width // LANES // 2 + 1) * 2 * SEG_DEV
    size = lax.axis_size("peak")
    pairs = ring_pairs(size)
    state_shapes = [((PAIRS, 2 * tokens), F32)] * 2 + [((PAIRS, HD, 2 * tokens), F32)]
    turned_shape = ((PAIRS, LANES, 2 * tokens), BF16)
    operands = (
        hidden_in[0], value_bins, mask_flags, segment_ids[0], bin_table[0], mask_vector,
    )
    operands = [pltpu.with_memory_space_constraint(operand, pltpu.HBM) for operand in operands]
    vmem = pl.BlockSpec(memory_space=pltpu.VMEM)
    first, second, summary = pl.pallas_call(
        embed_kernel,
        out_shape=[
            jax.ShapeDtypeStruct((cut * width // LANES + extra, LANES), BF16),
            jax.ShapeDtypeStruct((tokens - cut, width), BF16),
            jax.ShapeDtypeStruct((extra, LANES), BF16),
        ],
        in_specs=[pl.BlockSpec(memory_space=pltpu.HBM)] * len(operands),
        out_specs=[vmem] * 3,
        scratch_shapes=[pltpu.VMEM(operand.shape, operand.dtype) for operand in operands]
        + [pltpu.SemaphoreType.DMA((len(operands),))],
        compiler_params=pltpu.CompilerParams(vmem_limit_bytes=VMEM_BYTES),
        cost_estimate=pl.CostEstimate(flops=2**20, bytes_accessed=2**10, transcendentals=0),
    )(*operands)
    weights = [
        call(arrange_kernel, [(weight.shape, BF16)], 2**20, weight)[0]
        for weight in (qkv_weight, swapped(qkv_weight))
    ]
    out_there = swapped(out_weight)

    summary = swapped(summary)
    for step in range(size - 1):
        next_first = lax.ppermute(first, "peak", pairs)
        next_second = lax.ppermute(second, "peak", pairs)
        if step == 0:
            next_first, summary, *weights = after(next_first, summary, *weights)
            turned, *state = call(
                own_kernel, [turned_shape] + state_shapes, COST[0],
                first, second, next_first, summary, *weights,
            )
        else:
            state = call(
                middle_kernel, state_shapes, COST[1],
                second, next_first, summary, *weights, turned, *state,
            )
        if step < size - 2:
            next_second, *state = after(next_second, *state)
        first, second = next_first, next_second
        summary = swapped(first[first.shape[0] - extra :])
    (update,) = pl.pallas_call(
        last_kernel,
        out_shape=[jax.ShapeDtypeStruct((tokens, width), BF16)],
        in_specs=[pl.BlockSpec(memory_space=pltpu.VMEM)] * 10,
        out_specs=[pl.BlockSpec(memory_space=pltpu.VMEM)],
        scratch_shapes=[pltpu.VMEM((width, tokens), BF16)],
        compiler_params=pltpu.CompilerParams(vmem_limit_bytes=VMEM_BYTES),
        cost_estimate=pl.CostEstimate(flops=2**20, bytes_accessed=2**10, transcendentals=0),
    )(second, summary, *weights, turned, *state, out_weight, out_there)
    return update[None]


def solution(mesh):
    placed = (
        P("mod", ("dp", "peak"), None),
        P("mod", ("dp", "peak")),
        P("mod", ("dp", "peak")),
        P("mod", ("dp", "peak"), None),
        P("mod", None, None),
        P("mod", None),
        P("mod", None),
        P("mod", None),
    )
    return jax.shard_map(
        shards,
        mesh=mesh,
        in_specs=placed,
        out_specs=P("mod", ("dp", "peak"), None),
        check_vma=False,
    )
```

```python
import jax
import jax.numpy as jnp
from jax import lax
from jax.experimental import pallas as pl
from jax.experimental.pallas import tpu as pltpu
from jax.sharding import PartitionSpec as P

H = 16
HD = 64
SEG_DEV = 4
PAIRS = H // 2
LANES = 128
BF16 = jnp.bfloat16
F32 = jnp.float32
VMEM_BYTES = 24 * 2**20
NEVER = -1e30
COST = (2**28, 2**28)


def call(kernel, outs, flops, *operands):
    spec = pl.BlockSpec(memory_space=pltpu.VMEM)
    shapes = [jax.ShapeDtypeStruct(shape, dtype) for shape, dtype in outs]
    return pl.pallas_call(
        kernel,
        out_shape=shapes,
        in_specs=[spec] * len(operands),
        out_specs=[spec] * len(shapes),
        compiler_params=pltpu.CompilerParams(vmem_limit_bytes=VMEM_BYTES),
        cost_estimate=pl.CostEstimate(flops=flops, bytes_accessed=2**10, transcendentals=0),
    )(*operands)


def contract(left, right, left_dim, right_dim):
    return lax.dot_general(
        left, right, (((left_dim,), (right_dim,)), ((), ())), preferred_element_type=F32
    )


def embed_kernel(*refs):
    sources, (first, second, summary), copies, done = refs[:6], refs[6:9], refs[9:15], refs[15]
    moves = [
        pltpu.make_async_copy(source, copy, done.at[i])
        for i, (source, copy) in enumerate(zip(sources, copies))
    ]
    for move in moves:
        move.start()
    for move in moves[1:]:
        move.wait()
    hidden, bins, flags, segs, table, mask_row = copies
    tokens, width = hidden.shape
    half = width // 2
    cut = tokens // 2
    mod = lax.axis_index("mod")
    one_hot = (
        lax.broadcasted_iota(jnp.int32, (table.shape[0], tokens), 0) == bins[...]
    ).astype(BF16)
    flag_rows = jnp.broadcast_to((flags[...] == 1).astype(F32), (LANES, tokens))
    flag_cols = jnp.concatenate([jnp.transpose(flag_rows)] * (half // LANES), axis=1) > 0.5
    seg_rows = lax.broadcasted_iota(jnp.int32, (2 * SEG_DEV, tokens), 0)
    picks = (lax.rem(seg_rows, SEG_DEV) == segs[...]).astype(F32)
    counts = jnp.sum(picks, axis=1, keepdims=True)
    picks = picks.astype(BF16)
    is_mean = lax.broadcasted_iota(jnp.int32, (2 * SEG_DEV, half), 0) < SEG_DEV
    starts = [pl.multiple_of(lax.rem(mod + part, 2) * half, half) for part in range(2)]
    bin_parts = [contract(one_hot, table[:, pl.ds(start, half)], 0, 0) for start in starts]
    means = []
    moves[0].wait()
    for part, (start, bin_rows) in enumerate(zip(starts, bin_parts)):
        chosen = jnp.where(
            flag_cols,
            mask_row[:, pl.ds(start, half)].astype(F32),
            hidden[:, pl.ds(start, half)].astype(F32),
        )
        embedded = (chosen + bin_rows).astype(BF16)
        columns = pl.ds(part * half, half)
        for tile in range(half // LANES):
            at = (part * (half // LANES) + tile) * cut
            first[at : at + cut, :] = embedded[:cut, tile * LANES : (tile + 1) * LANES]
        second[:, columns] = embedded[cut:]
        means.append(contract(picks, embedded, 1, 0) / counts)
    both = jnp.where(is_mean, means[1], means[0])
    bias = jnp.broadcast_to(jnp.log(counts), (2 * SEG_DEV, LANES))
    tiles = [both[:, at : at + LANES] for at in range(0, half, LANES)]
    packed = jnp.concatenate(tiles + [bias], axis=0).astype(BF16)
    summary[...] = packed
    first[first.shape[0] - packed.shape[0] :, :] = packed


def arrange_kernel(weight, arranged):
    rows = weight.shape[0]
    width = H * HD
    low = lax.broadcasted_iota(jnp.int32, (rows, LANES), 1) < HD
    for pair in range(PAIRS):
        at = pair * 3 * LANES
        query_key, value_query, key_value = [
            weight[:, at + i * LANES : at + (i + 1) * LANES] for i in range(3)
        ]
        to = pair * LANES
        arranged[:, to : to + LANES] = jnp.where(low, query_key, value_query)
        arranged[:, width + to : width + to + LANES] = jnp.where(low, key_value, query_key)
        arranged[:, 2 * width + to : 2 * width + to + LANES] = jnp.where(
            low, value_query, key_value
        )


def project(rows, weight_here, weight_there, start, stop):
    half = rows.shape[1] // 2
    return contract(rows[:, :half], weight_here[:, start:stop], 1, 0) + contract(
        rows[:, half:], weight_there[:, start:stop], 1, 0
    )


def fold(rows, summary_bias, weight_here, weight_there, turned, old, new):
    width = H * HD
    count = rows.shape[0]
    key = project(rows, weight_here, weight_there, width, 2 * width).astype(BF16)
    low = lax.broadcasted_iota(jnp.int32, (HD, LANES), 1) < HD
    scores, folded = {}, {}

    def score(pair):
        found = contract(key[:, pair * LANES : (pair + 1) * LANES], turned[pair], 1, 0)
        if summary_bias is not None:
            edge = count - summary_bias.shape[0]
            found = jnp.concatenate([found[:edge], found[edge:] + summary_bias], axis=0)
        scores[pair] = found

    def weigh(pair):
        found = scores.pop(pair)
        top = jnp.max(found, axis=0, keepdims=True)
        if old is not None:
            top = jnp.maximum(top, old[0][pair : pair + 1, :])
        weights = jnp.exp(found - top)
        total = jnp.sum(weights, axis=0, keepdims=True)
        shrink = None
        if old is not None:
            shrink = jnp.exp(old[0][pair : pair + 1, :] - top)
            total = total + shrink * old[1][pair : pair + 1, :]
        folded[pair] = (weights.astype(BF16), top, total, shrink)

    def attend(pair):
        weights, top, total, shrink = folded.pop(pair)
        product = contract(value[pair * LANES : (pair + 1) * LANES], weights, 1, 0)
        summed = jnp.concatenate(
            [
                product[:HD, :LANES],
                product[HD:, LANES : 2 * LANES],
                jnp.where(low, product[:HD, 2 * LANES :], product[HD:, 2 * LANES :]),
            ],
            axis=1,
        )
        if old is not None:
            summed = summed + shrink * old[2][pair]
        new(pair, top, total, summed)

    score(0)
    score(1)
    value = project(rows, weight_here, weight_there, 2 * width, 3 * width)
    value = jnp.transpose(value).astype(BF16)
    for pair in range(PAIRS):
        if pair + 2 < PAIRS:
            score(pair + 2)
        weigh(pair)
        if pair >= 1:
            attend(pair - 1)
    attend(PAIRS - 1)


def tokens_of(first, width):
    count = width // LANES
    cut = (first.shape[0] - (count // 2 + 1) * 2 * SEG_DEV) // count
    return jnp.concatenate([first[tile * cut : (tile + 1) * cut, :] for tile in range(count)], axis=1)


def summaries_of(packed):
    rows = 2 * SEG_DEV
    tiles = packed[...].astype(F32)
    tiles = [tiles[at : at + rows] for at in range(0, packed.shape[0], rows)]
    turned = [jnp.concatenate([tile[SEG_DEV:], tile[:SEG_DEV]], axis=0) for tile in tiles[:-1]]
    means = jnp.concatenate(tiles[:-1] + turned, axis=1).astype(BF16)
    is_key = lax.broadcasted_iota(jnp.int32, (rows, 3 * LANES), 0) < SEG_DEV
    return means, jnp.where(is_key, jnp.concatenate([tiles[-1]] * 3, axis=1), NEVER)


def store_state(top_ref, total_ref, summed_ref):
    def store(pair, top, total, summed):
        top_ref[pair : pair + 1, :] = top
        total_ref[pair : pair + 1, :] = total
        summed_ref[pair] = summed

    return store


def own_kernel(
    first, second, arrived, summary, weight_here, weight_there,
    turned, top_ref, total_ref, summed_ref,
):
    cut, width = second.shape
    means, bias = summaries_of(summary)
    rows = jnp.concatenate(
        [tokens_of(first, width), second[...], tokens_of(arrived, width), means], axis=0
    )
    query = project(rows[: 2 * cut], weight_here, weight_there, 0, width).astype(BF16)
    query = query.astype(F32) * (float(HD) ** -0.5)
    zeros = jnp.zeros((HD, LANES), F32)
    for pair in range(PAIRS):
        flipped = jnp.transpose(query[:, pair * LANES : (pair + 1) * LANES])
        even, odd = flipped[:HD], flipped[HD:]
        gap = jnp.zeros((HD, HD), F32)
        turned[pair] = jnp.concatenate(
            [
                jnp.concatenate([zeros, odd[:, :LANES], gap, odd[:, LANES:]], axis=1),
                jnp.concatenate([even[:, :LANES], zeros, even[:, LANES:], gap], axis=1),
            ],
            axis=0,
        ).astype(BF16)
    fold(
        rows, bias, weight_here, weight_there, turned, None,
        store_state(top_ref, total_ref, summed_ref),
    )


def middle_kernel(
    second, first, summary, weight_here, weight_there, turned, top_in, total_in, summed_in,
    top_ref, total_ref, summed_ref,
):
    means, bias = summaries_of(summary)
    rows = jnp.concatenate([second[...], tokens_of(first, second.shape[1]), means], axis=0)
    fold(
        rows, bias, weight_here, weight_there, turned, (top_in, total_in, summed_in),
        store_state(top_ref, total_ref, summed_ref),
    )


def last_kernel(
    second, summary, weight_here, weight_there, turned, top_in, total_in, summed_in,
    out_here, out_there, update, attended,
):
    def finish(pair, top, total, summed):
        done = (summed * (1.0 / total)).astype(BF16)
        for odd in range(2):
            at = pair * LANES + odd * HD
            rest = 2 * LANES + odd * HD
            attended[at : at + HD, :] = jnp.concatenate(
                [done[:, odd * LANES : (odd + 1) * LANES], done[:, rest : rest + HD]], axis=1
            )

    means, bias = summaries_of(summary)
    fold(
        jnp.concatenate([second[...], means], axis=0), bias, weight_here, weight_there, turned,
        (top_in, total_in, summed_in), finish,
    )
    half = out_here.shape[0]
    mod = lax.axis_index("mod")
    here = attended[pl.ds(pl.multiple_of(mod * half, half), half), :]
    there = attended[pl.ds(pl.multiple_of((1 - mod) * half, half), half), :]
    update[...] = (
        contract(here, out_here[...], 0, 0) + contract(there, out_there[...], 0, 0)
    ).astype(BF16)


def ring_pairs(size):
    order = [0] + list(range(1, size, 2)) + list(reversed(range(2, size, 2)))
    return [(order[(i + 1) % size], order[i]) for i in range(size)]


def after(*values):
    return lax.optimization_barrier(values)


def swapped(value):
    return lax.ppermute(value, "mod", [(0, 1), (1, 0)])


def shards(
    hidden_in, value_bins, mask_flags, segment_ids, bin_table, mask_vector, qkv_weight, out_weight
):
    tokens, width = hidden_in.shape[1:]
    cut = tokens // 2
    extra = (width // LANES // 2 + 1) * 2 * SEG_DEV
    size = lax.axis_size("peak")
    pairs = ring_pairs(size)
    state_shapes = [((PAIRS, 2 * tokens), F32)] * 2 + [((PAIRS, HD, 2 * tokens), F32)]
    turned_shape = ((PAIRS, LANES, 2 * tokens), BF16)
    operands = (
        hidden_in[0], value_bins, mask_flags, segment_ids[0], bin_table[0], mask_vector,
    )
    operands = [pltpu.with_memory_space_constraint(operand, pltpu.HBM) for operand in operands]
    vmem = pl.BlockSpec(memory_space=pltpu.VMEM)
    first, second, summary = pl.pallas_call(
        embed_kernel,
        out_shape=[
            jax.ShapeDtypeStruct((cut * width // LANES + extra, LANES), BF16),
            jax.ShapeDtypeStruct((tokens - cut, width), BF16),
            jax.ShapeDtypeStruct((extra, LANES), BF16),
        ],
        in_specs=[pl.BlockSpec(memory_space=pltpu.HBM)] * len(operands),
        out_specs=[vmem] * 3,
        scratch_shapes=[pltpu.VMEM(operand.shape, operand.dtype) for operand in operands]
        + [pltpu.SemaphoreType.DMA((len(operands),))],
        compiler_params=pltpu.CompilerParams(vmem_limit_bytes=VMEM_BYTES),
        cost_estimate=pl.CostEstimate(flops=2**20, bytes_accessed=2**10, transcendentals=0),
    )(*operands)
    weights = [
        call(arrange_kernel, [(weight.shape, BF16)], 2**20, weight)[0]
        for weight in (qkv_weight, swapped(qkv_weight))
    ]
    out_there = swapped(out_weight)

    summary = swapped(summary)
    for step in range(size - 1):
        next_first = lax.ppermute(first, "peak", pairs)
        next_second = lax.ppermute(second, "peak", pairs)
        if step == 0:
            next_first, summary, *weights = after(next_first, summary, *weights)
            turned, *state = call(
                own_kernel, [turned_shape] + state_shapes, COST[0],
                first, second, next_first, summary, *weights,
            )
        else:
            state = call(
                middle_kernel, state_shapes, COST[1],
                second, next_first, summary, *weights, turned, *state,
            )
        if step < size - 2:
            next_second, *state = after(next_second, *state)
        first, second = next_first, next_second
        summary = swapped(first[first.shape[0] - extra :])
    (update,) = pl.pallas_call(
        last_kernel,
        out_shape=[jax.ShapeDtypeStruct((tokens, width), BF16)],
        in_specs=[pl.BlockSpec(memory_space=pltpu.VMEM)] * 10,
        out_specs=[pl.BlockSpec(memory_space=pltpu.VMEM)],
        scratch_shapes=[pltpu.VMEM((width, tokens), BF16)],
        compiler_params=pltpu.CompilerParams(vmem_limit_bytes=VMEM_BYTES),
        cost_estimate=pl.CostEstimate(flops=2**20, bytes_accessed=2**10, transcendentals=0),
    )(second, summary, *weights, turned, *state, out_weight, out_there)
    return update[None]


def solution(mesh):
    placed = (
        P("mod", ("dp", "peak"), None),
        P("mod", ("dp", "peak")),
        P("mod", ("dp", "peak")),
        P("mod", ("dp", "peak"), None),
        P("mod", None, None),
        P("mod", None),
        P("mod", None),
        P("mod", None),
    )
    return jax.shard_map(
        shards,
        mesh=mesh,
        in_specs=placed,
        out_specs=P("mod", ("dp", "peak"), None),
        check_vma=False,
    )
```

```python
import jax
import jax.numpy as jnp
from jax import lax
from jax.experimental import pallas as pl
from jax.experimental.pallas import tpu as pltpu
from jax.sharding import PartitionSpec as P

H = 16
HD = 64
SEG_DEV = 4
PAIRS = H // 2
LANES = 128
BF16 = jnp.bfloat16
F32 = jnp.float32
VMEM_BYTES = 24 * 2**20
NEVER = -1e30
COST = (2**28, 2**28)


def call(kernel, outs, flops, *operands):
    spec = pl.BlockSpec(memory_space=pltpu.VMEM)
    shapes = [jax.ShapeDtypeStruct(shape, dtype) for shape, dtype in outs]
    return pl.pallas_call(
        kernel,
        out_shape=shapes,
        in_specs=[spec] * len(operands),
        out_specs=[spec] * len(shapes),
        compiler_params=pltpu.CompilerParams(vmem_limit_bytes=VMEM_BYTES),
        cost_estimate=pl.CostEstimate(flops=flops, bytes_accessed=2**10, transcendentals=0),
    )(*operands)


def contract(left, right, left_dim, right_dim):
    return lax.dot_general(
        left, right, (((left_dim,), (right_dim,)), ((), ())), preferred_element_type=F32
    )


def embed_kernel(*refs):
    sources, (first, second, summary), copies, done = refs[:6], refs[6:9], refs[9:15], refs[15]
    moves = [
        pltpu.make_async_copy(source, copy, done.at[i])
        for i, (source, copy) in enumerate(zip(sources, copies))
    ]
    for move in moves:
        move.start()
    for move in moves[1:]:
        move.wait()
    hidden, bins, flags, segs, table, mask_row = copies
    tokens, width = hidden.shape
    half = width // 2
    cut = tokens // 2
    mod = lax.axis_index("mod")
    one_hot = (
        lax.broadcasted_iota(jnp.int32, (table.shape[0], tokens), 0) == bins[...]
    ).astype(BF16)
    flag_rows = jnp.broadcast_to((flags[...] == 1).astype(F32), (LANES, tokens))
    flag_cols = jnp.concatenate([jnp.transpose(flag_rows)] * (half // LANES), axis=1) > 0.5
    seg_rows = lax.broadcasted_iota(jnp.int32, (2 * SEG_DEV, tokens), 0)
    picks = (lax.rem(seg_rows, SEG_DEV) == segs[...]).astype(F32)
    counts = jnp.sum(picks, axis=1, keepdims=True)
    picks = picks.astype(BF16)
    is_mean = lax.broadcasted_iota(jnp.int32, (2 * SEG_DEV, half), 0) < SEG_DEV
    starts = [pl.multiple_of(lax.rem(mod + part, 2) * half, half) for part in range(2)]
    bin_parts = [contract(one_hot, table[:, pl.ds(start, half)], 0, 0) for start in starts]
    means = []
    moves[0].wait()
    for part, (start, bin_rows) in enumerate(zip(starts, bin_parts)):
        chosen = jnp.where(
            flag_cols,
            mask_row[:, pl.ds(start, half)].astype(F32),
            hidden[:, pl.ds(start, half)].astype(F32),
        )
        embedded = (chosen + bin_rows).astype(BF16)
        columns = pl.ds(part * half, half)
        for tile in range(half // LANES):
            at = (part * (half // LANES) + tile) * cut
            first[at : at + cut, :] = embedded[:cut, tile * LANES : (tile + 1) * LANES]
        second[:, columns] = embedded[cut:]
        means.append(contract(picks, embedded, 1, 0) / counts)
    both = jnp.where(is_mean, means[1], means[0])
    bias = jnp.broadcast_to(jnp.log(counts), (2 * SEG_DEV, LANES))
    tiles = [both[:, at : at + LANES] for at in range(0, half, LANES)]
    packed = jnp.concatenate(tiles + [bias], axis=0).astype(BF16)
    summary[...] = packed
    first[first.shape[0] - packed.shape[0] :, :] = packed


def arrange_kernel(weight, arranged):
    rows = weight.shape[0]
    width = H * HD
    low = lax.broadcasted_iota(jnp.int32, (rows, LANES), 1) < HD
    for pair in range(PAIRS):
        at = pair * 3 * LANES
        query_key, value_query, key_value = [
            weight[:, at + i * LANES : at + (i + 1) * LANES] for i in range(3)
        ]
        to = pair * LANES
        arranged[:, to : to + LANES] = jnp.where(low, query_key, value_query)
        arranged[:, width + to : width + to + LANES] = jnp.where(low, key_value, query_key)
        arranged[:, 2 * width + to : 2 * width + to + LANES] = jnp.where(
            low, value_query, key_value
        )


def project(rows, weight_here, weight_there, start, stop):
    half = rows.shape[1] // 2
    return contract(rows[:, :half], weight_here[:, start:stop], 1, 0) + contract(
        rows[:, half:], weight_there[:, start:stop], 1, 0
    )


def fold(rows, summary_bias, weight_here, weight_there, turned, old, new):
    width = H * HD
    count = rows.shape[0]
    key = project(rows, weight_here, weight_there, width, 2 * width).astype(BF16)
    low = lax.broadcasted_iota(jnp.int32, (HD, LANES), 1) < HD
    scores, folded = {}, {}

    def score(pair):
        found = contract(key[:, pair * LANES : (pair + 1) * LANES], turned[pair], 1, 0)
        if summary_bias is not None:
            edge = count - summary_bias.shape[0]
            found = jnp.concatenate([found[:edge], found[edge:] + summary_bias], axis=0)
        scores[pair] = found

    def weigh(pair):
        found = scores.pop(pair)
        top = jnp.max(found, axis=0, keepdims=True)
        if old is not None:
            top = jnp.maximum(top, old[0][pair : pair + 1, :])
        weights = jnp.exp(found - top)
        total = jnp.sum(weights, axis=0, keepdims=True)
        shrink = None
        if old is not None:
            shrink = jnp.exp(old[0][pair : pair + 1, :] - top)
            total = total + shrink * old[1][pair : pair + 1, :]
        folded[pair] = (weights.astype(BF16), top, total, shrink)

    def attend(pair):
        weights, top, total, shrink = folded.pop(pair)
        product = contract(value[pair * LANES : (pair + 1) * LANES], weights, 1, 0)
        summed = jnp.concatenate(
            [
                product[:HD, :LANES],
                product[HD:, LANES : 2 * LANES],
                jnp.where(low, product[:HD, 2 * LANES :], product[HD:, 2 * LANES :]),
            ],
            axis=1,
        )
        if old is not None:
            summed = summed + shrink * old[2][pair]
        new(pair, top, total, summed)

    score(0)
    score(1)
    score(2)
    value = project(rows, weight_here, weight_there, 2 * width, 3 * width)
    value = jnp.transpose(value).astype(BF16)
    for pair in range(PAIRS):
        if pair + 3 < PAIRS:
            score(pair + 3)
        weigh(pair)
        if pair >= 1:
            attend(pair - 1)
    attend(PAIRS - 1)


def tokens_of(first, width):
    count = width // LANES
    cut = (first.shape[0] - (count // 2 + 1) * 2 * SEG_DEV) // count
    return jnp.concatenate([first[tile * cut : (tile + 1) * cut, :] for tile in range(count)], axis=1)


def summaries_of(packed):
    rows = 2 * SEG_DEV
    tiles = packed[...].astype(F32)
    tiles = [tiles[at : at + rows] for at in range(0, packed.shape[0], rows)]
    turned = [jnp.concatenate([tile[SEG_DEV:], tile[:SEG_DEV]], axis=0) for tile in tiles[:-1]]
    means = jnp.concatenate(tiles[:-1] + turned, axis=1).astype(BF16)
    is_key = lax.broadcasted_iota(jnp.int32, (rows, 3 * LANES), 0) < SEG_DEV
    return means, jnp.where(is_key, jnp.concatenate([tiles[-1]] * 3, axis=1), NEVER)


def store_state(top_ref, total_ref, summed_ref):
    def store(pair, top, total, summed):
        top_ref[pair : pair + 1, :] = top
        total_ref[pair : pair + 1, :] = total
        summed_ref[pair] = summed

    return store


def own_kernel(
    first, second, arrived, summary, weight_here, weight_there,
    turned, top_ref, total_ref, summed_ref,
):
    cut, width = second.shape
    means, bias = summaries_of(summary)
    rows = jnp.concatenate(
        [tokens_of(first, width), second[...], tokens_of(arrived, width), means], axis=0
    )
    query = project(rows[: 2 * cut], weight_here, weight_there, 0, width).astype(BF16)
    query = query.astype(F32) * (float(HD) ** -0.5)
    zeros = jnp.zeros((HD, LANES), F32)
    for pair in range(PAIRS):
        flipped = jnp.transpose(query[:, pair * LANES : (pair + 1) * LANES])
        even, odd = flipped[:HD], flipped[HD:]
        gap = jnp.zeros((HD, HD), F32)
        turned[pair] = jnp.concatenate(
            [
                jnp.concatenate([zeros, odd[:, :LANES], gap, odd[:, LANES:]], axis=1),
                jnp.concatenate([even[:, :LANES], zeros, even[:, LANES:], gap], axis=1),
            ],
            axis=0,
        ).astype(BF16)
    fold(
        rows, bias, weight_here, weight_there, turned, None,
        store_state(top_ref, total_ref, summed_ref),
    )


def middle_kernel(
    second, first, summary, weight_here, weight_there, turned, top_in, total_in, summed_in,
    top_ref, total_ref, summed_ref,
):
    means, bias = summaries_of(summary)
    rows = jnp.concatenate([second[...], tokens_of(first, second.shape[1]), means], axis=0)
    fold(
        rows, bias, weight_here, weight_there, turned, (top_in, total_in, summed_in),
        store_state(top_ref, total_ref, summed_ref),
    )


def last_kernel(
    second, summary, weight_here, weight_there, turned, top_in, total_in, summed_in,
    out_here, out_there, update, attended,
):
    def finish(pair, top, total, summed):
        done = (summed * (1.0 / total)).astype(BF16)
        for odd in range(2):
            at = pair * LANES + odd * HD
            rest = 2 * LANES + odd * HD
            attended[at : at + HD, :] = jnp.concatenate(
                [done[:, odd * LANES : (odd + 1) * LANES], done[:, rest : rest + HD]], axis=1
            )

    means, bias = summaries_of(summary)
    fold(
        jnp.concatenate([second[...], means], axis=0), bias, weight_here, weight_there, turned,
        (top_in, total_in, summed_in), finish,
    )
    half = out_here.shape[0]
    mod = lax.axis_index("mod")
    here = attended[pl.ds(pl.multiple_of(mod * half, half), half), :]
    there = attended[pl.ds(pl.multiple_of((1 - mod) * half, half), half), :]
    update[...] = (
        contract(here, out_here[...], 0, 0) + contract(there, out_there[...], 0, 0)
    ).astype(BF16)


def ring_pairs(size):
    order = [0] + list(range(1, size, 2)) + list(reversed(range(2, size, 2)))
    return [(order[(i + 1) % size], order[i]) for i in range(size)]


def after(*values):
    return lax.optimization_barrier(values)


def swapped(value):
    return lax.ppermute(value, "mod", [(0, 1), (1, 0)])


def shards(
    hidden_in, value_bins, mask_flags, segment_ids, bin_table, mask_vector, qkv_weight, out_weight
):
    tokens, width = hidden_in.shape[1:]
    cut = tokens // 2
    extra = (width // LANES // 2 + 1) * 2 * SEG_DEV
    size = lax.axis_size("peak")
    pairs = ring_pairs(size)
    state_shapes = [((PAIRS, 2 * tokens), F32)] * 2 + [((PAIRS, HD, 2 * tokens), F32)]
    turned_shape = ((PAIRS, LANES, 2 * tokens), BF16)
    operands = (
        hidden_in[0], value_bins, mask_flags, segment_ids[0], bin_table[0], mask_vector,
    )
    operands = [pltpu.with_memory_space_constraint(operand, pltpu.HBM) for operand in operands]
    vmem = pl.BlockSpec(memory_space=pltpu.VMEM)
    first, second, summary = pl.pallas_call(
        embed_kernel,
        out_shape=[
            jax.ShapeDtypeStruct((cut * width // LANES + extra, LANES), BF16),
            jax.ShapeDtypeStruct((tokens - cut, width), BF16),
            jax.ShapeDtypeStruct((extra, LANES), BF16),
        ],
        in_specs=[pl.BlockSpec(memory_space=pltpu.HBM)] * len(operands),
        out_specs=[vmem] * 3,
        scratch_shapes=[pltpu.VMEM(operand.shape, operand.dtype) for operand in operands]
        + [pltpu.SemaphoreType.DMA((len(operands),))],
        compiler_params=pltpu.CompilerParams(vmem_limit_bytes=VMEM_BYTES),
        cost_estimate=pl.CostEstimate(flops=2**20, bytes_accessed=2**10, transcendentals=0),
    )(*operands)
    weights = [
        call(arrange_kernel, [(weight.shape, BF16)], 2**20, weight)[0]
        for weight in (qkv_weight, swapped(qkv_weight))
    ]
    out_there = swapped(out_weight)

    summary = swapped(summary)
    for step in range(size - 1):
        next_first = lax.ppermute(first, "peak", pairs)
        next_second = lax.ppermute(second, "peak", pairs)
        if step == 0:
            next_first, summary, *weights = after(next_first, summary, *weights)
            turned, *state = call(
                own_kernel, [turned_shape] + state_shapes, COST[0],
                first, second, next_first, summary, *weights,
            )
        else:
            state = call(
                middle_kernel, state_shapes, COST[1],
                second, next_first, summary, *weights, turned, *state,
            )
        if step < size - 2:
            next_second, *state = after(next_second, *state)
        first, second = next_first, next_second
        summary = swapped(first[first.shape[0] - extra :])
    (update,) = pl.pallas_call(
        last_kernel,
        out_shape=[jax.ShapeDtypeStruct((tokens, width), BF16)],
        in_specs=[pl.BlockSpec(memory_space=pltpu.VMEM)] * 10,
        out_specs=[pl.BlockSpec(memory_space=pltpu.VMEM)],
        scratch_shapes=[pltpu.VMEM((width, tokens), BF16)],
        compiler_params=pltpu.CompilerParams(vmem_limit_bytes=VMEM_BYTES),
        cost_estimate=pl.CostEstimate(flops=2**20, bytes_accessed=2**10, transcendentals=0),
    )(second, summary, *weights, turned, *state, out_weight, out_there)
    return update[None]


def solution(mesh):
    placed = (
        P("mod", ("dp", "peak"), None),
        P("mod", ("dp", "peak")),
        P("mod", ("dp", "peak")),
        P("mod", ("dp", "peak"), None),
        P("mod", None, None),
        P("mod", None),
        P("mod", None),
        P("mod", None),
    )
    return jax.shard_map(
        shards,
        mesh=mesh,
        in_specs=placed,
        out_specs=P("mod", ("dp", "peak"), None),
        check_vma=False,
    )
```

```python
import jax
import jax.numpy as jnp
from jax import lax
from jax.experimental import pallas as pl
from jax.experimental.pallas import tpu as pltpu
from jax.sharding import PartitionSpec as P

H = 16
HD = 64
SEG_DEV = 4
PAIRS = H // 2
LANES = 128
BF16 = jnp.bfloat16
F32 = jnp.float32
VMEM_BYTES = 24 * 2**20
NEVER = -1e30
COST = (2**28, 2**28)


def call(kernel, outs, flops, *operands):
    spec = pl.BlockSpec(memory_space=pltpu.VMEM)
    shapes = [jax.ShapeDtypeStruct(shape, dtype) for shape, dtype in outs]
    return pl.pallas_call(
        kernel,
        out_shape=shapes,
        in_specs=[spec] * len(operands),
        out_specs=[spec] * len(shapes),
        compiler_params=pltpu.CompilerParams(vmem_limit_bytes=VMEM_BYTES),
        cost_estimate=pl.CostEstimate(flops=flops, bytes_accessed=2**10, transcendentals=0),
    )(*operands)


def contract(left, right, left_dim, right_dim):
    return lax.dot_general(
        left, right, (((left_dim,), (right_dim,)), ((), ())), preferred_element_type=F32
    )


def embed_kernel(*refs):
    sources, (first, second, summary), copies, done = refs[:6], refs[6:9], refs[9:15], refs[15]
    moves = [
        pltpu.make_async_copy(source, copy, done.at[i])
        for i, (source, copy) in enumerate(zip(sources, copies))
    ]
    for move in moves:
        move.start()
    for move in moves[1:]:
        move.wait()
    hidden, bins, flags, segs, table, mask_row = copies
    tokens, width = hidden.shape
    half = width // 2
    cut = tokens // 2
    mod = lax.axis_index("mod")
    one_hot = (
        lax.broadcasted_iota(jnp.int32, (table.shape[0], tokens), 0) == bins[...]
    ).astype(BF16)
    flag_rows = jnp.broadcast_to((flags[...] == 1).astype(F32), (LANES, tokens))
    flag_cols = jnp.concatenate([jnp.transpose(flag_rows)] * (half // LANES), axis=1) > 0.5
    seg_rows = lax.broadcasted_iota(jnp.int32, (2 * SEG_DEV, tokens), 0)
    picks = (lax.rem(seg_rows, SEG_DEV) == segs[...]).astype(F32)
    counts = jnp.sum(picks, axis=1, keepdims=True)
    picks = picks.astype(BF16)
    is_mean = lax.broadcasted_iota(jnp.int32, (2 * SEG_DEV, half), 0) < SEG_DEV
    starts = [pl.multiple_of(lax.rem(mod + part, 2) * half, half) for part in range(2)]
    bin_parts = [contract(one_hot, table[:, pl.ds(start, half)], 0, 0) for start in starts]
    means = []
    moves[0].wait()
    for part, (start, bin_rows) in enumerate(zip(starts, bin_parts)):
        chosen = jnp.where(
            flag_cols,
            mask_row[:, pl.ds(start, half)].astype(F32),
            hidden[:, pl.ds(start, half)].astype(F32),
        )
        embedded = (chosen + bin_rows).astype(BF16)
        columns = pl.ds(part * half, half)
        for tile in range(half // LANES):
            at = (part * (half // LANES) + tile) * cut
            first[at : at + cut, :] = embedded[:cut, tile * LANES : (tile + 1) * LANES]
        second[:, columns] = embedded[cut:]
        means.append(contract(picks, embedded, 1, 0) / counts)
    both = jnp.where(is_mean, means[1], means[0])
    bias = jnp.broadcast_to(jnp.log(counts), (2 * SEG_DEV, LANES))
    tiles = [both[:, at : at + LANES] for at in range(0, half, LANES)]
    packed = jnp.concatenate(tiles + [bias], axis=0).astype(BF16)
    summary[...] = packed
    first[first.shape[0] - packed.shape[0] :, :] = packed


def arrange_kernel(weight, arranged):
    rows = weight.shape[0]
    width = H * HD
    low = lax.broadcasted_iota(jnp.int32, (rows, LANES), 1) < HD
    for pair in range(PAIRS):
        at = pair * 3 * LANES
        query_key, value_query, key_value = [
            weight[:, at + i * LANES : at + (i + 1) * LANES] for i in range(3)
        ]
        to = pair * LANES
        arranged[:, to : to + LANES] = jnp.where(low, query_key, value_query)
        arranged[:, width + to : width + to + LANES] = jnp.where(low, key_value, query_key)
        arranged[:, 2 * width + to : 2 * width + to + LANES] = jnp.where(
            low, value_query, key_value
        )


def project(rows, weight_here, weight_there, start, stop):
    half = rows.shape[1] // 2
    return contract(rows[:, :half], weight_here[:, start:stop], 1, 0) + contract(
        rows[:, half:], weight_there[:, start:stop], 1, 0
    )


def fold(rows, summary_bias, weight_here, weight_there, turned, old, new):
    width = H * HD
    count = rows.shape[0]
    key = project(rows, weight_here, weight_there, width, 2 * width).astype(BF16)
    low = lax.broadcasted_iota(jnp.int32, (HD, LANES), 1) < HD
    scores, folded = {}, {}

    def score(pair):
        found = contract(key[:, pair * LANES : (pair + 1) * LANES], turned[pair], 1, 0)
        if summary_bias is not None:
            edge = count - summary_bias.shape[0]
            found = jnp.concatenate([found[:edge], found[edge:] + summary_bias], axis=0)
        scores[pair] = found

    def weigh(pair):
        found = scores.pop(pair)
        top = jnp.max(found, axis=0, keepdims=True)
        if old is not None:
            top = jnp.maximum(top, old[0][pair : pair + 1, :])
        weights = jnp.exp(found - top)
        total = jnp.sum(weights, axis=0, keepdims=True)
        shrink = None
        if old is not None:
            shrink = jnp.exp(old[0][pair : pair + 1, :] - top)
            total = total + shrink * old[1][pair : pair + 1, :]
        folded[pair] = (weights.astype(BF16), top, total, shrink)

    def attend(pair):
        weights, top, total, shrink = folded.pop(pair)
        product = contract(value[pair * LANES : (pair + 1) * LANES], weights, 1, 0)
        summed = jnp.concatenate(
            [
                product[:HD, :LANES],
                product[HD:, LANES : 2 * LANES],
                jnp.where(low, product[:HD, 2 * LANES :], product[HD:, 2 * LANES :]),
            ],
            axis=1,
        )
        if old is not None:
            summed = summed + shrink * old[2][pair]
        new(pair, top, total, summed)

    score(0)
    score(1)
    value = project(rows, weight_here, weight_there, 2 * width, 3 * width)
    value = jnp.transpose(value).astype(BF16)
    for pair in range(PAIRS):
        if pair + 2 < PAIRS:
            score(pair + 2)
        if pair >= 1:
            attend(pair - 1)
        weigh(pair)
    attend(PAIRS - 1)


def tokens_of(first, width):
    count = width // LANES
    cut = (first.shape[0] - (count // 2 + 1) * 2 * SEG_DEV) // count
    return jnp.concatenate([first[tile * cut : (tile + 1) * cut, :] for tile in range(count)], axis=1)


def summaries_of(packed):
    rows = 2 * SEG_DEV
    tiles = packed[...].astype(F32)
    tiles = [tiles[at : at + rows] for at in range(0, packed.shape[0], rows)]
    turned = [jnp.concatenate([tile[SEG_DEV:], tile[:SEG_DEV]], axis=0) for tile in tiles[:-1]]
    means = jnp.concatenate(tiles[:-1] + turned, axis=1).astype(BF16)
    is_key = lax.broadcasted_iota(jnp.int32, (rows, 3 * LANES), 0) < SEG_DEV
    return means, jnp.where(is_key, jnp.concatenate([tiles[-1]] * 3, axis=1), NEVER)


def store_state(top_ref, total_ref, summed_ref):
    def store(pair, top, total, summed):
        top_ref[pair : pair + 1, :] = top
        total_ref[pair : pair + 1, :] = total
        summed_ref[pair] = summed

    return store


def own_kernel(
    first, second, arrived, summary, weight_here, weight_there,
    turned, top_ref, total_ref, summed_ref,
):
    cut, width = second.shape
    means, bias = summaries_of(summary)
    rows = jnp.concatenate(
        [tokens_of(first, width), second[...], tokens_of(arrived, width), means], axis=0
    )
    query = project(rows[: 2 * cut], weight_here, weight_there, 0, width).astype(BF16)
    query = query.astype(F32) * (float(HD) ** -0.5)
    zeros = jnp.zeros((HD, LANES), F32)
    for pair in range(PAIRS):
        flipped = jnp.transpose(query[:, pair * LANES : (pair + 1) * LANES])
        even, odd = flipped[:HD], flipped[HD:]
        gap = jnp.zeros((HD, HD), F32)
        turned[pair] = jnp.concatenate(
            [
                jnp.concatenate([zeros, odd[:, :LANES], gap, odd[:, LANES:]], axis=1),
                jnp.concatenate([even[:, :LANES], zeros, even[:, LANES:], gap], axis=1),
            ],
            axis=0,
        ).astype(BF16)
    fold(
        rows, bias, weight_here, weight_there, turned, None,
        store_state(top_ref, total_ref, summed_ref),
    )


def middle_kernel(
    second, first, summary, weight_here, weight_there, turned, top_in, total_in, summed_in,
    top_ref, total_ref, summed_ref,
):
    means, bias = summaries_of(summary)
    rows = jnp.concatenate([second[...], tokens_of(first, second.shape[1]), means], axis=0)
    fold(
        rows, bias, weight_here, weight_there, turned, (top_in, total_in, summed_in),
        store_state(top_ref, total_ref, summed_ref),
    )


def last_kernel(
    second, summary, weight_here, weight_there, turned, top_in, total_in, summed_in,
    out_here, out_there, update, attended,
):
    def finish(pair, top, total, summed):
        done = (summed * (1.0 / total)).astype(BF16)
        for odd in range(2):
            at = pair * LANES + odd * HD
            rest = 2 * LANES + odd * HD
            attended[at : at + HD, :] = jnp.concatenate(
                [done[:, odd * LANES : (odd + 1) * LANES], done[:, rest : rest + HD]], axis=1
            )

    means, bias = summaries_of(summary)
    fold(
        jnp.concatenate([second[...], means], axis=0), bias, weight_here, weight_there, turned,
        (top_in, total_in, summed_in), finish,
    )
    half = out_here.shape[0]
    mod = lax.axis_index("mod")
    here = attended[pl.ds(pl.multiple_of(mod * half, half), half), :]
    there = attended[pl.ds(pl.multiple_of((1 - mod) * half, half), half), :]
    update[...] = (
        contract(here, out_here[...], 0, 0) + contract(there, out_there[...], 0, 0)
    ).astype(BF16)


def ring_pairs(size):
    order = [0] + list(range(1, size, 2)) + list(reversed(range(2, size, 2)))
    return [(order[(i + 1) % size], order[i]) for i in range(size)]


def after(*values):
    return lax.optimization_barrier(values)


def swapped(value):
    return lax.ppermute(value, "mod", [(0, 1), (1, 0)])


def shards(
    hidden_in, value_bins, mask_flags, segment_ids, bin_table, mask_vector, qkv_weight, out_weight
):
    tokens, width = hidden_in.shape[1:]
    cut = tokens // 2
    extra = (width // LANES // 2 + 1) * 2 * SEG_DEV
    size = lax.axis_size("peak")
    pairs = ring_pairs(size)
    state_shapes = [((PAIRS, 2 * tokens), F32)] * 2 + [((PAIRS, HD, 2 * tokens), F32)]
    turned_shape = ((PAIRS, LANES, 2 * tokens), BF16)
    operands = (
        hidden_in[0], value_bins, mask_flags, segment_ids[0], bin_table[0], mask_vector,
    )
    operands = [pltpu.with_memory_space_constraint(operand, pltpu.HBM) for operand in operands]
    vmem = pl.BlockSpec(memory_space=pltpu.VMEM)
    first, second, summary = pl.pallas_call(
        embed_kernel,
        out_shape=[
            jax.ShapeDtypeStruct((cut * width // LANES + extra, LANES), BF16),
            jax.ShapeDtypeStruct((tokens - cut, width), BF16),
            jax.ShapeDtypeStruct((extra, LANES), BF16),
        ],
        in_specs=[pl.BlockSpec(memory_space=pltpu.HBM)] * len(operands),
        out_specs=[vmem] * 3,
        scratch_shapes=[pltpu.VMEM(operand.shape, operand.dtype) for operand in operands]
        + [pltpu.SemaphoreType.DMA((len(operands),))],
        compiler_params=pltpu.CompilerParams(vmem_limit_bytes=VMEM_BYTES),
        cost_estimate=pl.CostEstimate(flops=2**20, bytes_accessed=2**10, transcendentals=0),
    )(*operands)
    weights = [
        call(arrange_kernel, [(weight.shape, BF16)], 2**20, weight)[0]
        for weight in (qkv_weight, swapped(qkv_weight))
    ]
    out_there = swapped(out_weight)

    summary = swapped(summary)
    for step in range(size - 1):
        next_first = lax.ppermute(first, "peak", pairs)
        next_second = lax.ppermute(second, "peak", pairs)
        if step == 0:
            next_first, summary, *weights = after(next_first, summary, *weights)
            turned, *state = call(
                own_kernel, [turned_shape] + state_shapes, COST[0],
                first, second, next_first, summary, *weights,
            )
        else:
            state = call(
                middle_kernel, state_shapes, COST[1],
                second, next_first, summary, *weights, turned, *state,
            )
        if step < size - 2:
            next_second, *state = after(next_second, *state)
        first, second = next_first, next_second
        summary = swapped(first[first.shape[0] - extra :])
    (update,) = pl.pallas_call(
        last_kernel,
        out_shape=[jax.ShapeDtypeStruct((tokens, width), BF16)],
        in_specs=[pl.BlockSpec(memory_space=pltpu.VMEM)] * 10,
        out_specs=[pl.BlockSpec(memory_space=pltpu.VMEM)],
        scratch_shapes=[pltpu.VMEM((width, tokens), BF16)],
        compiler_params=pltpu.CompilerParams(vmem_limit_bytes=VMEM_BYTES),
        cost_estimate=pl.CostEstimate(flops=2**20, bytes_accessed=2**10, transcendentals=0),
    )(second, summary, *weights, turned, *state, out_weight, out_there)
    return update[None]


def solution(mesh):
    placed = (
        P("mod", ("dp", "peak"), None),
        P("mod", ("dp", "peak")),
        P("mod", ("dp", "peak")),
        P("mod", ("dp", "peak"), None),
        P("mod", None, None),
        P("mod", None),
        P("mod", None),
        P("mod", None),
    )
    return jax.shard_map(
        shards,
        mesh=mesh,
        in_specs=placed,
        out_specs=P("mod", ("dp", "peak"), None),
        check_vma=False,
    )
```
